32 devices in a mesh: grp: 8 (over z, x), box: 4 (over y, core).
Axes of the slice: x: 2, y: 2, z: 4, core: 2. Of those that a mesh axis runs over, the one named last changes fastest.
Arguments:
- source_term: float32 [53, 8, 8, 256], P(None, 'grp', 'box'), may hold values from -24 to 24
- diffusion: float32 [53], replicated, may hold values from 0.1 to 2
- stoich: float32 [53, 325], replicated, may hold values from -0.3125 to 0.3125
- orders: float32 [325, 53], replicated, may hold values from -0.875 to 0.875
- rates: float32 [325, 8, 8, 256], P(None, 'grp', 'box'), may hold values from 0.1 to 1
- precond: bfloat16 [53, 53, 8, 8, 256], P(None, None, 'grp', 'box'), may hold values from -1 to 1
- coarse_field: float32 [53, 8, 1024], P(None, 'grp', 'box'), may hold values from -6 to 6
- neighbours: int32 [8, 4], replicated, may hold values from -1 to 7, as said below
- ghost_list: int32 [8, 4, 160], P(None, 'box'), may hold values from -1 to 2047, as said below
- average_list: int32 [8, 4], P(None, 'box'), may hold values from 0 to 31, as said below
Outputs:
- correction: float32 [53, 8, 8, 256], P(None, 'grp', 'box')
- coarse_update: float32 [53, 8, 1024], P(None, 'grp', 'box')
The draws below stay inside these ranges and needn't reach their ends.
Inputs may be any that keep to these rules, and one draw needn't show every extreme that they name: Column g sits at one position of a grid 4 columns wide and 2 rows tall, each position taken once; neighbours[g, 0] and neighbours[g, 1] are the columns before and after it in its grid row, neighbours[g, 2] and neighbours[g, 3] the ones in the grid rows below and above, -1 at the grid's edge. The relation is symmetric: neighbours[neighbours[g, f], f xor 1] = g. `ghost_list`: an entry is -1 exactly where its face meets another fine sub-box: the lower x face for b > 0, the upper x face for b < 3, side face f where neighbours[g, f] >= 0. Every other entry is o * 256 + c, coarse cell c of the patch of column o at the same box index. `average_list`: entry o * 4 + j names block j of the patch of column o at the same box index; at each box index the 8 entries are distinct.
All inputs are finite; a program needn't handle non-finite values.
Results may differ from the reference program's by a relative error of at most 0.0007.
Values sent between devices are 32-bit elements; how exact they have to be, the bound alone decides.
A program may use at most 64 MiB of HBM per device.

```python
import math
import jax
import jax.numpy as jnp
from jax import lax

S = 53
R = 325
FS = 16
CX = 2
ITERS = 4
CBLK = 4
GROUPS = 8
BOXES = 4
FACE = 256
XFACE_C = 64
SIDE_C = 8
GHOSTS = 160
BLOCK_C = 64
COARSE = 256


def column_layout(key):
    order = jax.random.permutation(key, GROUPS).astype(jnp.int32)
    spot = jnp.argsort(order, stable=True).astype(jnp.int32)
    column = spot % 4
    line = spot // 4
    targets = jnp.stack([spot - 1, spot + 1, spot - 4, spot + 4], axis=1)
    inside = jnp.stack([column > 0, column < 3, line > 0, line < GROUPS // 4 - 1], axis=1)
    found = order[jnp.clip(targets, 0, GROUPS - 1)]
    return jnp.where(inside, found, -1).astype(jnp.int32)


def draw_neighbours(key, part):
    return column_layout(key)


def draw_ghost_list(key, part):
    links = column_layout(key)
    key = jax.random.fold_in(key, 11)
    first_key, second_key = jax.random.split(key)
    owner = jax.random.randint(first_key, (GROUPS, BOXES, GHOSTS), 0, GROUPS)
    cell = jax.random.randint(second_key, (GROUPS, BOXES, GHOSTS), 0, COARSE)
    source = owner * COARSE + cell
    slot = jnp.arange(GHOSTS)
    box_ids = jnp.arange(BOXES)[None, :, None]
    side_face = jnp.clip((slot - 2 * XFACE_C) // SIDE_C, 0, 3)
    side_link = jnp.take(links, side_face, axis=1)[:, None, :]
    slot_b = slot[None, None, :]
    shared = jnp.where(slot_b < XFACE_C, box_ids > 0, jnp.where(slot_b < 2 * XFACE_C, box_ids < BOXES - 1, side_link >= 0))
    source = jnp.where(shared, -1, source)
    source = source.at[0, 0, 0].set(GROUPS * COARSE - 1)
    return source.astype(jnp.int32)


def draw_average_list(key, part):
    key = jax.random.fold_in(key, 23)

    def one_column(box_id):
        box_key = jax.random.fold_in(key, box_id)
        first_key, second_key, third_key = jax.random.split(box_key, 3)
        heavy = jax.random.randint(first_key, (), 0, GROUPS)
        heavy = jnp.where(box_id == 0, GROUPS - 1, jnp.where(box_id == BOXES - 1, 0, heavy))
        slots = jax.random.permutation(second_key, GROUPS * CBLK).astype(jnp.int32)
        ranking = jnp.where(slots // CBLK == heavy, 0, 1)
        chosen = slots[jnp.argsort(ranking, stable=True)][:GROUPS]
        return chosen[jax.random.permutation(third_key, GROUPS)]
    table = jax.vmap(one_column)(jnp.arange(BOXES))
    return jnp.transpose(table).astype(jnp.int32)


def draw_precond(key, part):
    key = jax.random.fold_in(key, 5)
    identity = (jnp.arange(S)[:, None] == jnp.arange(S)[None, :])[:, :, None, None]

    def one_group(group_id):
        group_key = jax.random.fold_in(key, group_id)
        first_key, second_key = jax.random.split(group_key)
        scale = jnp.exp(jax.random.uniform(first_key, (S, 1, BOXES * CX, FACE), jnp.float32, math.log(0.1), 0.0))
        noise = jnp.clip(jax.random.normal(second_key, (S, S, BOXES * CX, FACE), jnp.float32), -4.0, 4.0)
        return jnp.where(identity, scale, 0.1 * scale * noise).astype(jnp.bfloat16)
    stacked = lax.map(one_group, jnp.arange(GROUPS))
    return jnp.moveaxis(stacked, 0, 2)


def level_of(own_key, shape, cuts, low, largest):
    gain = 1.0
    for position, shards_of in cuts:
        steps = jax.random.uniform(jax.random.fold_in(jax.random.fold_in(own_key, 6), position), (shards_of,), jnp.float32, low / len(cuts), largest / len(cuts))
        gain = gain * jnp.repeat(jnp.exp(steps), shape[position] // shards_of).reshape((-1,) + (1,) * (len(shape) - 1 - position))
    return gain


def gaussian(own_key, dims, width, reach, cuts=(), kind=jnp.bfloat16):
    drawn = jax.random.normal(own_key, dims, jnp.float32) * width
    if len(cuts) > 0:
        drawn = level_of(own_key, dims, cuts, -0.22, 0.18) * drawn
    return jnp.clip(drawn, min=-reach, max=reach).astype(kind)


def setup_inputs(seed: int = 0) -> dict:
    arg_keys = jax.random.split(jax.random.key(seed), 11)
    return {
        "source_term": gaussian(arg_keys[0], (S, GROUPS, BOXES * CX, FACE), 4.0, 24.0, ((1, 8), (2, 4)), jnp.float32),
        "diffusion": jnp.clip(jnp.exp(jax.random.uniform(arg_keys[1], (S,), jnp.float32, math.log(0.1), math.log(2.0))), 0.1, 2.0),
        "stoich": gaussian(arg_keys[2], (S, R), R ** -0.5, 0.3125, (), jnp.float32),
        "orders": gaussian(arg_keys[3], (R, S), S ** -0.5, 0.875, (), jnp.float32),
        "rates": jnp.clip(jnp.exp(math.log(1.0) - 2.3025851 * jax.random.uniform(arg_keys[4], (R, GROUPS, BOXES * CX, FACE), jnp.float32) ** level_of(arg_keys[4], (R, GROUPS, BOXES * CX, FACE), ((1, 8), (2, 4)), -0.2, 0.2)), 0.1, 1.0),
        "precond": draw_precond(jax.random.fold_in(arg_keys[10], 71), 0),
        "coarse_field": gaussian(arg_keys[6], (S, GROUPS, BOXES * COARSE), 1.0, 6.0, ((1, 8), (2, 4)), jnp.float32),
        "neighbours": draw_neighbours(jax.random.fold_in(arg_keys[10], 71), 0),
        "ghost_list": draw_ghost_list(jax.random.fold_in(arg_keys[10], 71), 0),
        "average_list": draw_average_list(jax.random.fold_in(arg_keys[10], 71), 0),
    }


EXACT = lax.Precision.HIGHEST

def face_planes(core, side):
    return (core[..., :side], core[..., -side:], core[..., 0::side], core[..., side - 1::side])

def neighbour_sum(core, x_lower, x_upper, sides, side):
    padded = jnp.concatenate([x_lower[..., None, :], core, x_upper[..., None, :]], axis=-2)
    total = padded[..., :-2, :] + padded[..., 2:, :]
    total = total + jnp.concatenate([core[..., side:], sides[1]], axis=-1)
    total = total + jnp.concatenate([sides[0], core[..., :-side]], axis=-1)
    column = jnp.arange(core.shape[-1]) % side
    blank = jnp.zeros(core.shape[:-1] + (1,), core.dtype)
    ahead = jnp.concatenate([core[..., 1:], blank], axis=-1)
    behind = jnp.concatenate([blank, core[..., :-1]], axis=-1)
    total = total + jnp.where(column == side - 1, jnp.repeat(sides[3], side, axis=-1), ahead)
    total = total + jnp.where(column == 0, jnp.repeat(sides[2], side, axis=-1), behind)
    return total

def least_squares(columns, beta):
    count = len(columns)
    target = [beta] + [jnp.zeros_like(beta)] * count
    rotations = []
    upper = []
    for j in range(count):
        entries = list(columns[j])
        for i in range(j):
            cosine_part, sine_part = rotations[i]
            first = cosine_part * entries[i] + sine_part * entries[i + 1]
            second = cosine_part * entries[i + 1] - sine_part * entries[i]
            entries[i] = first
            entries[i + 1] = second
        radius = jnp.sqrt(entries[j] * entries[j] + entries[j + 1] * entries[j + 1])
        cosine_part = entries[j] / radius
        sine_part = entries[j + 1] / radius
        rotations.append((cosine_part, sine_part))
        entries[j] = radius
        target[j + 1] = -sine_part * target[j]
        target[j] = cosine_part * target[j]
        upper.append(entries[:j + 1])
    result = [None] * count
    for j in reversed(range(count)):
        running = target[j]
        for k in range(j + 1, count):
            running = running - upper[k][j] * result[k]
        result[j] = running / upper[j][j]
    return result

def reference(source_term, diffusion, stoich, orders, rates, precond, coarse_field, neighbours, ghost_list, average_list):
    shape = (S, GROUPS, BOXES, CX, FACE)
    half = FS // 2
    diffuse = diffusion[:, None, None, None, None]
    face_ids = jnp.arange(FACE)
    x_index = face_ids // FS // 2 * half + face_ids % FS // 2
    side_ids = jnp.arange(CX * FS)
    side_index = (side_ids // FS // 2 * half + side_ids % FS // 2).reshape(CX, FS)
    flat_coarse = coarse_field.reshape(S, GROUPS * BOXES * COARSE)
    owner = ghost_list // COARSE
    cell = ghost_list % COARSE
    box_ids = jnp.arange(BOXES)[None, :, None]
    location = jnp.where(ghost_list >= 0, owner * (BOXES * COARSE) + box_ids * COARSE + cell, 0).astype(jnp.int32)
    values = jnp.where(ghost_list[None] >= 0, jnp.take(flat_coarse, location, axis=1), 0.0)
    lower_x = values[..., :XFACE_C][..., x_index]
    upper_x = values[..., XFACE_C:2 * XFACE_C][..., x_index]
    sides = tuple((values[..., 2 * XFACE_C + f * SIDE_C:2 * XFACE_C + (f + 1) * SIDE_C][..., side_index] for f in range(4)))
    boundary = diffuse * neighbour_sum(jnp.zeros(shape, jnp.float32), lower_x, upper_x, sides, FS)
    right = source_term.reshape(shape) + boundary
    linked = neighbours >= 0
    partner = jnp.maximum(neighbours, 0).astype(jnp.int32)
    reaction = rates.reshape(R, -1)
    inverse = jnp.moveaxis(precond, 2, 0)

    def ghosts_of(field):
        planes = face_planes(field, FS)
        opposite = (planes[1], planes[0], planes[3], planes[2])
        return tuple((jnp.where(linked[None, :, f, None, None, None], jnp.take(opposite[f], partner[:, f], axis=1), 0.0) for f in range(4)))

    def operate(field):
        blank = jnp.zeros((S, GROUPS, 1, FACE), jnp.float32)
        x_low = jnp.concatenate([blank, field[:, :, :-1, -1]], axis=2)
        x_high = jnp.concatenate([field[:, :, 1:, 0], blank], axis=2)
        beside_all = neighbour_sum(field, x_low, x_high, ghosts_of(field), FS)
        progress = jnp.dot(orders, field.reshape(S, -1), precision=EXACT)
        chemistry = jnp.dot(stoich, reaction * progress, precision=EXACT).reshape(shape)
        return field + diffuse * (6.0 * field - beside_all) - chemistry

    def apply_block(pair):
        matrix, vector = pair
        return jnp.einsum('ijxc,jxc->ixc', matrix.astype(jnp.float32), vector, precision=EXACT)

    def precondition(field):
        moved = jnp.moveaxis(field.reshape(S, GROUPS, BOXES * CX, FACE), 1, 0)
        result = lax.map(apply_block, (inverse, moved))
        return jnp.moveaxis(result, 0, 1).reshape(shape)
    beta = jnp.sqrt(jnp.sum(right * right))
    basis = [right / beta]
    directions = []
    columns = []
    for j in range(ITERS):
        direction = precondition(basis[j])
        directions.append(direction)
        image = operate(direction)
        summed = jnp.stack([jnp.sum(basis[i] * image) for i in range(j + 1)])
        heights = [summed[i] for i in range(j + 1)]
        for i in range(j + 1):
            image = image - heights[i] * basis[i]
        length = jnp.sqrt(jnp.sum(image * image))
        columns.append(heights + [length])
        if j + 1 < ITERS:
            basis.append(image / length)
    weights = least_squares(columns, beta)
    correction = sum((weights[j] * directions[j] for j in range(ITERS)))
    pieces = correction.reshape(S, GROUPS, BOXES, CX // 2, 2, half, 2, half, 2)
    averaged = (lax.optimization_barrier(jnp.sum(pieces, axis=(4, 6, 8))) * 0.125).reshape(S, GROUPS, BOXES, BLOCK_C)
    blocks = coarse_field.reshape(S, GROUPS, BOXES, CBLK, BLOCK_C).transpose(0, 1, 3, 2, 4)
    blocks = blocks.reshape(S, GROUPS * CBLK, BOXES, BLOCK_C)
    box_grid = jnp.broadcast_to(jnp.arange(BOXES, dtype=jnp.int32)[None, :], (GROUPS, BOXES))
    blocks = blocks.at[:, average_list, box_grid].set(averaged)
    updated = blocks.reshape(S, GROUPS, CBLK, BOXES, BLOCK_C).transpose(0, 1, 3, 2, 4).reshape(S, GROUPS, BOXES * COARSE)
    return (correction.reshape(S, GROUPS, BOXES * CX, FACE), updated)
```

```python
import functools

import jax
import jax.numpy as jnp
from jax import lax
from jax.experimental import pallas as pl
from jax.experimental.pallas import tpu as pltpu
from jax.sharding import PartitionSpec as P

ITERS = 4
SP = 64
ROWS = 56
RP = 384
LANES = 128
MESH = pl.DeviceIdType.MESH
F32 = jnp.float32
BF16 = jnp.bfloat16


def least_squares(columns, beta):
    count = len(columns)
    target = [beta] + [jnp.zeros_like(beta)] * count
    rotations = []
    upper = []
    for j in range(count):
        entries = list(columns[j])
        for i in range(j):
            cosine_part, sine_part = rotations[i]
            first = cosine_part * entries[i] + sine_part * entries[i + 1]
            second = cosine_part * entries[i + 1] - sine_part * entries[i]
            entries[i] = first
            entries[i + 1] = second
        radius = jnp.sqrt(entries[j] * entries[j] + entries[j + 1] * entries[j + 1])
        cosine_part = entries[j] / radius
        sine_part = entries[j + 1] / radius
        rotations.append((cosine_part, sine_part))
        entries[j] = radius
        target[j + 1] = -sine_part * target[j]
        target[j] = cosine_part * target[j]
        upper.append(entries[: j + 1])
    result = [None] * count
    for j in reversed(range(count)):
        running = target[j]
        for k in range(j + 1, count):
            running = running - upper[k][j] * result[k]
        result[j] = running / upper[j][j]
    return result


def split(x, parts):
    pieces = []
    for _ in range(parts - 1):
        piece = x.astype(BF16)
        pieces.append(piece)
        x = x - piece.astype(F32)
    pieces.append(x.astype(BF16))
    return pieces


def dot(a, b):
    return jnp.dot(a, b, preferred_element_type=F32)


def exact_dot(x, ones, parts):
    rows = x.shape[0]
    product = dot(jnp.concatenate(split(x, parts), axis=0), ones)
    return sum(product[i * rows : (i + 1) * rows] for i in range(parts))


def iota(shape, dim):
    return lax.broadcasted_iota(jnp.int32, shape, dim)


def cell_of(index):
    k, l = index >> 7, index & 127
    return k >> 1, ((k & 1) << 3) + (l >> 4), l & 15


def on_face(face, t, y, z):
    return (
        ((face == 0) & (y == 0) & (z == t))
        | ((face == 1) & (y == 15) & (z == t))
        | ((face == 2) & (z == 0) & (y == t))
        | ((face == 3) & (z == 15) & (y == t))
    )


def ones_where(condition):
    return jnp.where(condition, 1.0, 0.0).astype(BF16)


def padded(x):
    return jnp.concatenate([x, jnp.zeros((SP - x.shape[0], x.shape[1]), F32)], axis=0)


def fields(x):
    return [x[:, k * LANES : (k + 1) * LANES] for k in range(4)]


def kernel(
    groups, boxes, species, reactions,
    neighbours, average_list, ghosts, source, diffusion, stoich, orders, rates, coarse, precond,
    correction_out, coarse_out,
    raw, wide, even, odd, applied, direct, basis, rate, stage, order_cat, stoich_cat, pick, spread,
    ghost_send, ghost_recv, plane_send, plane_recv, x_recv, red_send, red_recv, mean_send, mean_recv,
    load_sem, ghost_ssem, ghost_rsem, plane_ssem, plane_rsem, x_ssem, x_rsem,
    red_ssem, red_rsem, mean_ssem, mean_rsem,
):
    g = lax.axis_index("grp")
    b = lax.axis_index("box")
    load = pltpu.make_async_copy(precond, raw, load_sem)
    load.start()
    barrier = pltpu.get_barrier_semaphore()

    def grp_peer(k):
        return (lax.rem(g + k, groups), b)

    def box_peer(k):
        return (g, lax.rem(b + k, boxes))

    for k in range(1, groups):
        pl.semaphore_signal(barrier, inc=1, device_id=grp_peer(k), device_id_type=MESH)
    for k in range(1, boxes):
        pl.semaphore_signal(barrier, inc=1, device_id=box_peer(k), device_id_type=MESH)

    def remote(src, dst, ssem, rsem, device):
        return pltpu.make_async_remote_copy(
            src_ref=src, dst_ref=dst, send_sem=ssem, recv_sem=rsem,
            device_id=device, device_id_type=MESH,
        )

    stage[...] = jnp.zeros_like(stage)
    stage[0:species, 0:256] = coarse[...]
    patch = jnp.concatenate(split(stage[:, 0:256], 3), axis=0)
    cell = iota((256, LANES), 0) + g * 256

    def chosen(k):
        wanted = ghosts[pl.ds(lax.rem(g + k, groups), 1), :]
        got = dot(patch, ones_where(cell == wanted))
        return got[0:SP] + got[SP : 2 * SP] + got[2 * SP :]

    for k in range(1, groups):
        ghost_send[k - 1] = chosen(k)[0:ROWS]
    own_ghosts = chosen(0)
    pl.semaphore_wait(barrier, groups + boxes - 2)
    ghost_copies = [
        remote(ghost_send.at[k - 1], ghost_recv.at[k - 1], ghost_ssem.at[k - 1],
               ghost_rsem.at[k - 1], grp_peer(k))
        for k in range(1, groups)
    ]
    for copy in ghost_copies:
        copy.start()

    even[...] = jnp.zeros_like(even)
    odd[...] = jnp.zeros_like(odd)
    applied[...] = jnp.zeros_like(applied)
    rate[...] = jnp.zeros_like(rate)
    for x in range(2):
        for ct in range(2):
            k = 2 * x + ct
            rate[0:reactions, k * LANES : (k + 1) * LANES] = rates[
                pl.ds(2 * ct + x, reactions, stride=4), :
            ]
    order_cat[...] = jnp.zeros_like(order_cat)
    order_cat[0:reactions, 0:species] = orders[...]
    whole = order_cat[...]
    high = whole.astype(BF16).astype(F32)
    low = whole - high
    order_parts = jnp.concatenate([high + pltpu.roll(low, 64, 1), high], axis=1).astype(BF16)
    stage[...] = jnp.zeros_like(stage)
    stage[0:species, 0:reactions] = stoich[...]
    whole = stage[:, 0:RP]
    stoich_high, stoich_low = split(whole, 2)
    stoich_cat[0:SP, :] = stoich_high
    stoich_cat[SP : 2 * SP, :] = stoich_low
    x, y, z = cell_of(iota((512, LANES), 0))
    slot = iota((512, LANES), 1)
    pick[...] = ones_where(((slot >> 4 & 1) == x) & on_face(slot >> 5, slot & 15, y, z))
    x, y, z = cell_of(iota((LANES, 512), 1))
    slot = iota((LANES, 512), 0)
    spread[...] = ones_where(((slot >> 4 & 1) == x) & on_face(slot >> 5, slot & 15, y, z))
    end = jnp.where(b == 0, 0, 1)
    behind_x = (slot < 64) & (x == end) & (((y >> 1) << 3) + (z >> 1) == slot)
    past = slot - 64
    face = past >> 3
    t = jnp.where(face < 2, z, y)
    behind_side = (slot >= 64) & (slot < 96) & ((t >> 1) == (past & 7)) & on_face(face, t, y, z)
    coarse_spread = ones_where(behind_x | behind_side)

    load.wait()
    count = species * species * 4
    chunk = 432
    steps = count // chunk

    def widen(i, carry):
        at = pl.multiple_of(i * chunk, 16)
        wide[pl.ds(at, chunk), :] = raw[pl.ds(at, chunk), :].astype(F32)
        return carry

    lax.fori_loop(0, steps, widen, 0)
    tail = steps * chunk
    wide[tail:, :] = jnp.zeros((wide.shape[0] - tail, LANES), F32)
    wide[tail:count, :] = raw[tail:count, :].astype(F32)

    diffuse = jnp.concatenate([padded(diffusion[...])] * 4, axis=1)
    stage[...] = jnp.zeros_like(stage)
    for x in range(2):
        for ct in range(2):
            k = 2 * x + ct
            stage[0:species, k * LANES : (k + 1) * LANES] = source[
                pl.ds(2 * ct + x, species, stride=4), :
            ]
    for copy in ghost_copies:
        copy.wait_recv()
    values = own_ghosts[0:ROWS]
    for k in range(1, groups):
        values = values + ghost_recv[k - 1]
    basis[0] = stage[...] + diffuse * exact_dot(padded(values), coarse_spread, 3)

    half = species // 2

    def apply_inverse(v):
        for x in range(2):
            for ct in range(2):
                part = v[0:ROWS, (2 * x + ct) * LANES : (2 * x + ct + 1) * LANES]
                even[pl.ds(2 * ct + x, ROWS, stride=4), :] = part
                odd[pl.ds(4 + 2 * ct + x, ROWS, stride=4), :] = part
        rows = 4 * species + 4
        low_half = iota((8, LANES), 0) < 4

        def product(at, vector):
            p = (wide[pl.ds(pl.multiple_of(at, 8), rows), :] * vector[0:rows, :]).reshape(
                rows // 8, 8, LANES
            )
            parts = [p[i] for i in range(rows // 8)]
            while len(parts) > 1:
                pairs = [a + c for a, c in zip(parts[0::2], parts[1::2])]
                parts = pairs + ([parts[-1]] if len(parts) % 2 else [])
            return parts[0] + pltpu.roll(parts[0], 4, 0)

        def pair(m, carry):
            at = m * (8 * species)
            applied[pl.ds(pl.multiple_of(m * 8, 8), 8), :] = jnp.where(
                low_half, product(at, even), product(at + 4 * species - 4, odd)
            )
            return carry

        lax.fori_loop(0, half, pair, 0)
        applied[8 * half : 8 * half + 8, :] = jnp.where(
            low_half, product(half * 8 * species, even), 0.0
        )
        return [
            padded(applied[pl.ds(2 * ct + x, ROWS, stride=4), :])
            for x in range(2)
            for ct in range(2)
        ]

    lane = iota((16, LANES), 1)
    wide_lane = iota((SP, LANES), 1)
    links = [neighbours[g, f] for f in range(4)]

    def rolled(x, shift):
        shift = shift % LANES
        return pltpu.roll(x, shift, 1) if shift else x

    def side_messages(flat):
        planes = exact_dot(flat, pick[...], 2)
        packed = []
        for f in range(4):
            total = jnp.zeros((16, LANES), F32)
            for q in range(4):
                rows = planes[16 * q : 16 * q + 16]
                total = jnp.where((lane >> 5) == q, rolled(rows, 32 * (q - f)), total)
            packed.append(total)
        for k in range(1, groups):
            peer = lax.rem(g + k, groups)
            message = jnp.zeros((16, LANES), F32)
            for f in range(4):
                message = jnp.where(links[f] == peer, packed[f], message)
            plane_send[k - 1] = message

    def side_ghosts():
        found = [jnp.zeros((16, LANES), F32)] * 4
        for k in range(1, groups):
            peer = lax.rem(g + groups - k, groups)
            message = plane_recv[k - 1]
            found = [
                jnp.where(links[f] == peer, message, found[f]) for f in range(4)
            ]
        rows = []
        for q in range(4):
            total = jnp.zeros((16, LANES), F32)
            for f in range(4):
                total = jnp.where((lane >> 5) == f, rolled(found[f], 32 * (f - q)), total)
            rows.append(total)
        return exact_dot(jnp.concatenate(rows, axis=0), spread[...], 2)

    def inner_sum(d):
        result = []
        zero = jnp.zeros((SP, LANES), F32)
        z = wide_lane & 15
        for x in range(2):
            plane = d[2 * x : 2 * x + 2]
            up = [rolled(p, -16) for p in plane]
            down = [rolled(p, 16) for p in plane]
            for ct in range(2):
                own = plane[ct]
                total = d[2 * (1 - x) + ct]
                total = total + jnp.where(z == 15, 0.0, rolled(own, -1))
                total = total + jnp.where(z == 0, 0.0, rolled(own, 1))
                total = total + jnp.where(wide_lane >= 112, up[1] if ct == 0 else zero, up[ct])
                total = total + jnp.where(wide_lane < 16, down[0] if ct == 1 else zero, down[ct])
                result.append(total)
        return result

    def row_of(a, c):
        p = a * c
        p = p[:, 0:128] + p[:, 128:256] + p[:, 256:384] + p[:, 384:512]
        return jnp.sum(p, axis=0, keepdims=True)

    def all_reduce(rows, turn):
        at = turn % 2
        row_id = iota((8, LANES), 0)
        tile = jnp.zeros((8, LANES), F32)
        for i, row in enumerate(rows):
            tile = jnp.where(row_id == i, row, tile)
        first = 0
        for stage_id, (size, peer) in enumerate(((boxes, box_peer), (groups, grp_peer))):
            red_send[at, stage_id] = tile
            copies = [
                remote(red_send.at[at, stage_id], red_recv.at[at, first + k - 1],
                       red_ssem.at[at, first + k - 1], red_rsem.at[at, first + k - 1], peer(k))
                for k in range(1, size)
            ]
            for copy in copies:
                copy.start()
            for copy in copies:
                copy.wait_recv()
            for k in range(1, size):
                tile = tile + red_recv[at, first + k - 1]
            for copy in copies:
                copy.wait_send()
            first += size - 1
        sums = jnp.sum(tile, axis=1, keepdims=True)
        return [sums[i : i + 1] for i in range(len(rows))]

    for copy in ghost_copies:
        copy.wait_send()

    squares = []
    lengths = []
    columns = []
    for j in range(ITERS):
        d = apply_inverse(basis[j])
        for k in range(4):
            direct[j, k] = d[k]
        up = remote(direct.at[j, 2:4, 0:ROWS], x_recv.at[0], x_ssem.at[0], x_rsem.at[0],
                    (g, lax.rem(b + 1, boxes)))
        down = remote(direct.at[j, 0:2, 0:ROWS], x_recv.at[1], x_ssem.at[1], x_rsem.at[1],
                      (g, lax.rem(b + boxes - 1, boxes)))
        pl.when(b < boxes - 1)(up.start)
        pl.when(b > 0)(down.start)
        flat = jnp.concatenate(d, axis=1)
        side_messages(flat)
        plane_copies = [
            remote(plane_send.at[k - 1], plane_recv.at[k - 1], plane_ssem.at[k - 1],
                   plane_rsem.at[k - 1], grp_peer(k))
            for k in range(1, groups)
        ]
        for copy in plane_copies:
            copy.start()

        d_high, d_low = split(flat, 2)
        d_cat = jnp.concatenate([d_high, d_high, d_low, jnp.zeros_like(d_low)], axis=0)
        progress = rate[...] * dot(order_parts, d_cat)
        q_high, q_low = split(progress, 2)
        both = dot(stoich_cat[...], q_high)
        chemistry = both[0:SP] + both[SP:] + dot(stoich_cat[0:SP, :], q_low)
        inner = jnp.concatenate(inner_sum(d), axis=1)
        image = flat + diffuse * (6.0 * flat - inner) - chemistry

        pl.when(b > 0)(up.wait_recv)
        pl.when(b < boxes - 1)(down.wait_recv)
        zero = jnp.zeros((ROWS, LANES), F32)
        outer = [padded(jnp.where(b > 0, x_recv[0, ct], zero)) for ct in range(2)]
        outer += [padded(jnp.where(b < boxes - 1, x_recv[1, ct], zero)) for ct in range(2)]
        for copy in plane_copies:
            copy.wait_recv()
        image = image - diffuse * (jnp.concatenate(outer, axis=1) + side_ghosts())

        known = [basis[i] for i in range(j + 1)]
        rows = [row_of(known[j], known[j])] + [row_of(v, image) for v in known]
        sums = all_reduce(rows, j)
        pl.when(b < boxes - 1)(up.wait_send)
        pl.when(b > 0)(down.wait_send)
        for copy in plane_copies:
            copy.wait_send()
        squares.append(sums[0])
        lengths.append(jnp.sqrt(sums[0]))
        columns.append([sums[1 + i] / (lengths[i] * lengths[j]) for i in range(j + 1)])
        for i in range(j + 1):
            image = image - (sums[1 + i] / squares[i]) * known[i]
        basis[j + 1] = image / lengths[j]

    last = basis[ITERS]
    lengths.append(jnp.sqrt(all_reduce([row_of(last, last)], ITERS)[0]))
    for j in range(ITERS):
        columns[j].append(lengths[j + 1])
    weights = least_squares(columns, lengths[0])
    scales = [weights[j] / lengths[j] for j in range(ITERS)]
    total = [sum(scales[j] * direct[j, k] for j in range(ITERS)) for k in range(4)]
    cell = iota((256, LANES), 0)
    slot = iota((256, LANES), 1) & 63
    to_slot = (((((cell >> 7) << 3) + ((cell & 127) >> 4)) >> 1) << 3) + ((cell & 15) >> 1)
    pair_sum = jnp.concatenate([total[0] + total[2], total[1] + total[3]], axis=1)
    mean = exact_dot(pair_sum, ones_where(to_slot == slot), 3)[0:ROWS] * 0.125
    mean_send[...] = mean
    mean_copies = [
        remote(mean_send, mean_recv.at[k - 1], mean_ssem.at[k - 1], mean_rsem.at[k - 1], grp_peer(k))
        for k in range(1, groups)
    ]
    for copy in mean_copies:
        copy.start()
    for x in range(2):
        for ct in range(2):
            correction_out[pl.ds(2 * ct + x, species, stride=4), :] = total[2 * x + ct][0:species]
    for copy in mean_copies:
        copy.wait_recv()
    left = iota((ROWS, LANES), 1) < 64
    stage[...] = jnp.zeros_like(stage)
    stage[0:species, 0:256] = coarse[...]
    for c in range(2):
        block = stage[0:ROWS, c * LANES : (c + 1) * LANES]
        for k in range(groups):
            entry = average_list[lax.rem(g + groups - k, groups), 0] - (4 * g + 2 * c)
            message = mean if k == 0 else mean_recv[k - 1]
            block = jnp.where((left & (entry == 0)) | (~left & (entry == 1)), message, block)
        coarse_out[:, c * LANES : (c + 1) * LANES] = block[0:species]
    for copy in mean_copies:
        copy.wait_send()


def on_device(
    groups, boxes,
    source_term, diffusion, stoich, orders, rates, precond, coarse_field,
    neighbours, ghost_list, average_list,
):
    species = source_term.shape[0]
    reactions = rates.shape[0]

    def rows_of(x):
        lead = x.shape[:-3]
        x = x.reshape(lead + (2, 2, LANES))
        n = len(lead)
        x = x.transpose(tuple(range(n)) + (n + 1, n, n + 2))
        return x.reshape(-1, LANES)

    b = lax.axis_index("box")
    lists = ghost_list[:, 0, :]
    ghosts = jnp.concatenate(
        [
            jnp.where(b == 0, lists[:, 0:64], lists[:, 64:128]),
            lists[:, 128:160],
            jnp.full((groups, 32), -1, jnp.int32),
        ],
        axis=1,
    )
    vmem = pl.BlockSpec(memory_space=pltpu.VMEM)
    smem = pl.BlockSpec(memory_space=pltpu.SMEM)
    count = 4 * species * species
    dma = pltpu.SemaphoreType.DMA
    reds = groups + boxes - 2
    correction, updated = pl.pallas_call(
        functools.partial(kernel, groups, boxes, species, reactions),
        out_shape=(
            jax.ShapeDtypeStruct((4 * species, LANES), F32),
            jax.ShapeDtypeStruct((species, 256), F32),
        ),
        in_specs=[smem, smem] + [vmem] * 7 + [pl.BlockSpec(memory_space=pl.ANY)],
        out_specs=(vmem, vmem),
        scratch_shapes=[
            pltpu.VMEM((count, LANES), BF16),
            pltpu.VMEM((count + 4, LANES), F32),
            pltpu.VMEM((224, LANES), F32),
            pltpu.VMEM((232, LANES), F32),
            pltpu.VMEM((224, LANES), F32),
            pltpu.VMEM((ITERS, 4, SP, LANES), F32),
            pltpu.VMEM((ITERS + 1, SP, 512), F32),
            pltpu.VMEM((RP, 512), F32),
            pltpu.VMEM((SP, 512), F32),
            pltpu.VMEM((RP, LANES), F32),
            pltpu.VMEM((2 * SP, RP), BF16),
            pltpu.VMEM((512, LANES), BF16),
            pltpu.VMEM((LANES, 512), BF16),
            pltpu.VMEM((groups - 1, ROWS, LANES), F32),
            pltpu.VMEM((groups - 1, ROWS, LANES), F32),
            pltpu.VMEM((groups - 1, 16, LANES), F32),
            pltpu.VMEM((groups - 1, 16, LANES), F32),
            pltpu.VMEM((2, 2, ROWS, LANES), F32),
            pltpu.VMEM((2, 2, 8, LANES), F32),
            pltpu.VMEM((2, reds, 8, LANES), F32),
            pltpu.VMEM((ROWS, LANES), F32),
            pltpu.VMEM((groups - 1, ROWS, LANES), F32),
            dma,
            dma((groups - 1,)),
            dma((groups - 1,)),
            dma((groups - 1,)),
            dma((groups - 1,)),
            dma((2,)),
            dma((2,)),
            dma((2, reds)),
            dma((2, reds)),
            dma((groups - 1,)),
            dma((groups - 1,)),
        ],
        compiler_params=pltpu.CompilerParams(
            collective_id=0, has_side_effects=True, vmem_limit_bytes=40 * 1024 * 1024
        ),
        name="gmres",
    )(
        neighbours,
        average_list,
        ghosts,
        rows_of(source_term),
        jnp.broadcast_to(diffusion[:, None], (species, LANES)),
        stoich,
        orders,
        rows_of(rates),
        coarse_field.reshape(species, 256),
        rows_of(precond),
    )
    correction = correction.reshape(species, 2, 2, LANES).transpose(0, 2, 1, 3)
    return (
        correction.reshape(species, 1, 2, 256),
        updated.reshape(species, 1, 256),
    )


def solution(mesh):
    placed = (
        P(None, "grp", "box", None),
        P(),
        P(),
        P(),
        P(None, "grp", "box", None),
        P(None, None, "grp", "box", None),
        P(None, "grp", "box"),
        P(),
        P(None, "box", None),
        P(None, "box"),
    )
    return jax.shard_map(
        functools.partial(on_device, mesh.shape["grp"], mesh.shape["box"]),
        mesh=mesh,
        in_specs=placed,
        out_specs=(P(None, "grp", "box", None), P(None, "grp", "box")),
        check_vma=False,
    )
```

```python
import functools

import jax
import jax.numpy as jnp
from jax import lax
from jax.experimental import pallas as pl
from jax.experimental.pallas import tpu as pltpu
from jax.sharding import PartitionSpec as P

ITERS = 4
SP = 64
ROWS = 56
RP = 384
LANES = 128
MESH = pl.DeviceIdType.MESH
F32 = jnp.float32
BF16 = jnp.bfloat16


def rotated(columns, beta):
    count = len(columns)
    target = [beta] + [jnp.zeros_like(beta)] * (count - 1)
    rotations = []
    upper = []
    for j in range(count):
        entries = list(columns[j])
        for i in range(j):
            cosine_part, sine_part = rotations[i]
            first = cosine_part * entries[i] + sine_part * entries[i + 1]
            second = cosine_part * entries[i + 1] - sine_part * entries[i]
            entries[i] = first
            entries[i + 1] = second
        upper.append(entries)
        if j + 1 == count:
            return upper, target, entries[j]
        radius = jnp.sqrt(entries[j] * entries[j] + entries[j + 1] * entries[j + 1])
        cosine_part = entries[j] / radius
        sine_part = entries[j + 1] / radius
        rotations.append((cosine_part, sine_part))
        entries[j] = radius
        target[j + 1] = -sine_part * target[j]
        target[j] = cosine_part * target[j]


def back_substitute(upper, target, final):
    count = len(upper)
    result = [None] * (count - 1) + [final]
    for j in reversed(range(count - 1)):
        running = target[j]
        for k in range(j + 1, count):
            running = running - upper[k][j] * result[k]
        result[j] = running / upper[j][j]
    return result


def split(x, parts):
    pieces = []
    for _ in range(parts - 1):
        piece = x.astype(BF16)
        pieces.append(piece)
        x = x - piece.astype(F32)
    pieces.append(x.astype(BF16))
    return pieces


def dot(a, b):
    return jnp.dot(a, b, preferred_element_type=F32)


def exact_dot(x, ones, parts):
    rows = x.shape[0]
    product = dot(jnp.concatenate(split(x, parts), axis=0), ones)
    return sum(product[i * rows : (i + 1) * rows] for i in range(parts))


def iota(shape, dim):
    return lax.broadcasted_iota(jnp.int32, shape, dim)


def cell_of(index):
    k, l = index >> 7, index & 127
    return k >> 1, ((k & 1) << 3) + (l >> 4), l & 15


def on_face(face, t, y, z):
    return (
        ((face == 0) & (y == 0) & (z == t))
        | ((face == 1) & (y == 15) & (z == t))
        | ((face == 2) & (z == 0) & (y == t))
        | ((face == 3) & (z == 15) & (y == t))
    )


def ones_where(condition):
    return jnp.where(condition, 1.0, 0.0).astype(BF16)


def padded(x):
    return jnp.concatenate([x, jnp.zeros((SP - x.shape[0], x.shape[1]), F32)], axis=0)


def fields(x):
    return [x[:, k * LANES : (k + 1) * LANES] for k in range(4)]


def kernel(
    groups, boxes, species, reactions,
    neighbours, average_list, ghost_list, source, diffusion, stoich, orders, rates, coarse, precond,
    correction_out, coarse_out,
    raw, wide, even, odd, applied, direct, images, basis, rate, stage, tall, stoich_cat, pick, spread,
    lists, wanted_cells, source_raw, diffusion_raw, stoich_raw, orders_raw, rates_raw, coarse_raw, flow, patch_new,
    x_send, ghost_send, ghost_recv, plane_send, plane_recv, x_recv, red_send, red_recv,
    mean_send, mean_recv,
    load_sem, ghost_ssem, ghost_rsem, plane_ssem, plane_rsem, x_ssem, x_rsem,
    red_ssem, red_rsem, mean_ssem, mean_rsem,
):
    g = lax.axis_index("grp")
    b = lax.axis_index("box")
    barrier = pltpu.get_barrier_semaphore()

    def grp_peer(k):
        return (lax.rem(g + k, groups), b)

    def box_peer(k):
        return (g, lax.rem(b + k, boxes))

    for k in range(1, groups):
        pl.semaphore_signal(barrier, inc=1, device_id=grp_peer(k), device_id_type=MESH)
    for k in range(1, boxes):
        pl.semaphore_signal(barrier, inc=1, device_id=box_peer(k), device_id_type=MESH)

    def remote(src, dst, ssem, rsem, device):
        return pltpu.make_async_remote_copy(
            src_ref=src, dst_ref=dst, send_sem=ssem, recv_sem=rsem,
            device_id=device, device_id_type=MESH,
        )

    loads = [
        pltpu.make_async_copy(src, dst, load_sem.at[i])
        for i, (src, dst) in enumerate((
            (ghost_list.at[:, 0, :], lists),
            (coarse.at[:, 0, :], coarse_raw),
            (precond.reshape(4 * species * species, LANES), raw),
            (rates.reshape(4 * reactions, LANES), rates_raw),
            (orders, orders_raw),
            (stoich, stoich_raw),
            (diffusion, diffusion_raw),
            (source.reshape(4 * species, LANES), source_raw),
        ))
    ]
    for load in loads:
        load.start()

    stage[...] = jnp.zeros_like(stage)
    loads[0].wait()
    loads[1].wait()
    stage[0:species, 0:256] = coarse_raw[...]
    x_slots = lists[:, 0:LANES]
    x_slots = jnp.where(b == 0, x_slots, pltpu.roll(x_slots, 64, 1))
    side_slots = jnp.concatenate(
        [
            jnp.full((groups, 64), -1, jnp.int32),
            lists[:, LANES : LANES + 32],
            jnp.full((groups, 32), -1, jnp.int32),
        ],
        axis=1,
    )
    wanted_cells[...] = jnp.where(iota((groups, LANES), 1) < 64, x_slots, side_slots)
    patch = jnp.concatenate(split(stage[:, 0:256], 3), axis=0)
    cell = iota((256, LANES), 0) + g * 256

    def chosen(k):
        wanted = wanted_cells[pl.ds(lax.rem(g + k, groups), 1), :]
        got = dot(patch, ones_where(cell == wanted))
        return got[0:SP] + got[SP : 2 * SP] + got[2 * SP :]

    for k in range(1, groups):
        ghost_send[k - 1] = chosen(k)[0:ROWS]
    own_ghosts = chosen(0)
    pl.semaphore_wait(barrier, groups + boxes - 2)
    ghost_copies = [
        remote(ghost_send.at[k - 1], ghost_recv.at[k - 1], ghost_ssem.at[k - 1],
               ghost_rsem.at[k - 1], grp_peer(k))
        for k in range(1, groups)
    ]
    for copy in ghost_copies:
        copy.start()

    even[...] = jnp.zeros_like(even)
    odd[...] = jnp.zeros_like(odd)
    applied[...] = jnp.zeros_like(applied)
    rate[...] = jnp.zeros_like(rate)
    for load in loads[3:]:
        load.wait()
    for x in range(2):
        for ct in range(2):
            k = 2 * x + ct
            rate[0:reactions, k * LANES : (k + 1) * LANES] = rates_raw[
                pl.ds(2 * ct + x, reactions, stride=4), :
            ]
    tall[...] = jnp.zeros_like(tall)
    tall[0:species, 0:reactions] = orders_raw[...]
    whole = tall[...].T
    high = whole.astype(BF16).astype(F32)
    low = whole - high
    order_parts = jnp.concatenate([high + pltpu.roll(low, 64, 1), high], axis=1).astype(BF16)
    stage[...] = jnp.zeros_like(stage)
    stage[0:species, 0:reactions] = stoich_raw[...]
    whole = stage[:, 0:RP]
    stoich_high, stoich_low = split(whole, 2)
    stoich_cat[0:SP, :] = stoich_high
    stoich_cat[SP : 2 * SP, :] = stoich_low
    x, y, z = cell_of(iota((512, LANES), 0))
    slot = iota((512, LANES), 1)
    pick[...] = ones_where(((slot >> 4 & 1) == x) & on_face(slot >> 5, slot & 15, y, z))
    x, y, z = cell_of(iota((LANES, 512), 1))
    slot = iota((LANES, 512), 0)
    spread[...] = ones_where(((slot >> 4 & 1) == x) & on_face(slot >> 5, slot & 15, y, z))
    end = jnp.where(b == 0, 0, 1)
    behind_x = (slot < 64) & (x == end) & (((y >> 1) << 3) + (z >> 1) == slot)
    past = slot - 64
    face = past >> 3
    t = jnp.where(face < 2, z, y)
    behind_side = (slot >= 64) & (slot < 96) & ((t >> 1) == (past & 7)) & on_face(face, t, y, z)
    coarse_spread = ones_where(behind_x | behind_side)

    loads[2].wait()
    count = species * species * 4
    chunk = 432
    steps = count // chunk

    def widen(i, carry):
        at = pl.multiple_of(i * chunk, 16)
        wide[pl.ds(at, chunk), :] = raw[pl.ds(at, chunk), :].astype(F32)
        return carry

    lax.fori_loop(0, steps, widen, 0)
    tail = steps * chunk
    wide[tail:, :] = jnp.zeros((wide.shape[0] - tail, LANES), F32)
    wide[tail:count, :] = raw[tail:count, :].astype(F32)

    tall[0:8, 0:LANES] = jnp.zeros((8, LANES), F32)
    tall[0:1, 0:species] = diffusion_raw[...]
    same = iota((SP, LANES), 0) == iota((SP, LANES), 1)
    diffuse = jnp.sum(jnp.where(same, tall[0:1, 0:LANES], 0.0), axis=1, keepdims=True)
    diffuse = jnp.broadcast_to(diffuse, (SP, 512))
    stage[...] = jnp.zeros_like(stage)
    for x in range(2):
        for ct in range(2):
            k = 2 * x + ct
            stage[0:species, k * LANES : (k + 1) * LANES] = source_raw[
                pl.ds(2 * ct + x, species, stride=4), :
            ]
    for copy in ghost_copies:
        copy.wait_recv()
    values = own_ghosts[0:ROWS]
    for k in range(1, groups):
        values = values + ghost_recv[k - 1]
    basis[0] = stage[...] + diffuse * exact_dot(padded(values), coarse_spread, 3)

    half = species // 2

    def apply_inverse(v):
        for x in range(2):
            for ct in range(2):
                part = v[0:ROWS, (2 * x + ct) * LANES : (2 * x + ct + 1) * LANES]
                even[pl.ds(2 * ct + x, ROWS, stride=4), :] = part
                odd[pl.ds(4 + 2 * ct + x, ROWS, stride=4), :] = part
        rows = 4 * species + 4
        low_half = iota((8, LANES), 0) < 4

        def product(at, vector):
            p = (wide[pl.ds(pl.multiple_of(at, 8), rows), :] * vector[0:rows, :]).reshape(
                rows // 8, 8, LANES
            )
            parts = [p[i] for i in range(rows // 8)]
            while len(parts) > 1:
                pairs = [a + c for a, c in zip(parts[0::2], parts[1::2])]
                parts = pairs + ([parts[-1]] if len(parts) % 2 else [])
            return parts[0] + pltpu.roll(parts[0], 4, 0)

        def pair(m, carry):
            at = m * (8 * species)
            applied[pl.ds(pl.multiple_of(m * 8, 8), 8), :] = jnp.where(
                low_half, product(at, even), product(at + 4 * species - 4, odd)
            )
            return carry

        def two_pairs(m, carry):
            return pair(2 * m + 1, pair(2 * m, carry))

        lax.fori_loop(0, half // 2, two_pairs, 0)
        if half % 2:
            pair(half - 1, 0)
        applied[8 * half : 8 * half + 8, :] = jnp.where(
            low_half, product(half * 8 * species, even), 0.0
        )
        return [
            padded(applied[pl.ds(2 * ct + x, ROWS, stride=4), :])
            for x in range(2)
            for ct in range(2)
        ]

    lane = iota((16, LANES), 1)
    wide_lane = iota((SP, LANES), 1)
    links = [neighbours[f, g] for f in range(4)]

    def rolled(x, shift):
        shift = shift % LANES
        return pltpu.roll(x, shift, 1) if shift else x

    def side_messages(flat, at):
        planes = exact_dot(flat, pick[...], 2)
        packed = []
        for f in range(4):
            total = jnp.zeros((16, LANES), F32)
            for q in range(4):
                rows = planes[16 * q : 16 * q + 16]
                total = jnp.where((lane >> 5) == q, rolled(rows, 32 * (q - f)), total)
            packed.append(total)
        for k in range(1, groups):
            peer = lax.rem(g + k, groups)
            message = jnp.zeros((16, LANES), F32)
            for f in range(4):
                message = jnp.where(links[f] == peer, packed[f], message)
            plane_send[at, k - 1] = message

    def side_ghosts(at):
        found = [jnp.zeros((16, LANES), F32)] * 4
        for k in range(1, groups):
            peer = lax.rem(g + groups - k, groups)
            message = plane_recv[at, k - 1]
            found = [
                jnp.where(links[f] == peer, message, found[f]) for f in range(4)
            ]
        rows = []
        for q in range(4):
            total = jnp.zeros((16, LANES), F32)
            for f in range(4):
                total = jnp.where((lane >> 5) == f, rolled(found[f], 32 * (f - q)), total)
            rows.append(total)
        return exact_dot(jnp.concatenate(rows, axis=0), spread[...], 2)

    def inner_sum(d):
        result = []
        zero = jnp.zeros((SP, LANES), F32)
        z = wide_lane & 15
        for x in range(2):
            plane = d[2 * x : 2 * x + 2]
            up = [rolled(p, -16) for p in plane]
            down = [rolled(p, 16) for p in plane]
            for ct in range(2):
                own = plane[ct]
                total = d[2 * (1 - x) + ct]
                total = total + jnp.where(z == 15, 0.0, rolled(own, -1))
                total = total + jnp.where(z == 0, 0.0, rolled(own, 1))
                total = total + jnp.where(wide_lane >= 112, up[1] if ct == 0 else zero, up[ct])
                total = total + jnp.where(wide_lane < 16, down[0] if ct == 1 else zero, down[ct])
                result.append(total)
        return result

    def row_of(a, c):
        p = a * c
        p = p[:, 0:128] + p[:, 128:256] + p[:, 256:384] + p[:, 384:512]
        return jnp.sum(p, axis=0, keepdims=True)

    def reduce_stage(tile, turn, stage_id):
        at = turn % 2
        first, size, peer = ((0, boxes, box_peer), (boxes - 1, groups, grp_peer))[stage_id]
        red_send[at, stage_id] = tile
        copies = [
            remote(red_send.at[at, stage_id], red_recv.at[at, first + k - 1],
                   red_ssem.at[at, first + k - 1], red_rsem.at[at, first + k - 1], peer(k))
            for k in range(1, size)
        ]
        for copy in copies:
            copy.start()

        def finish():
            total = tile
            for copy in copies:
                copy.wait_recv()
            for k in range(1, size):
                total = total + red_recv[at, first + k - 1]
            for copy in copies:
                copy.wait_send()
            return total

        return finish

    def reduce_rows(rows, turn):
        row_id = iota((8, LANES), 0)
        tile = jnp.zeros((8, LANES), F32)
        for i, row in enumerate(rows):
            tile = jnp.where(row_id == i, row, tile)
        return reduce_stage(tile, turn, 0)

    def sums_of(tile):
        return jnp.sum(tile, axis=1, keepdims=True)

    def send_halo(v, turn):
        at = turn % 2
        d = apply_inverse(v)
        for k in range(4):
            x_send[at, k] = d[k]
        up = remote(x_send.at[at, 2:4, 0:ROWS], x_recv.at[at, 0], x_ssem.at[at, 0],
                    x_rsem.at[at, 0], (g, lax.rem(b + 1, boxes)))
        down = remote(x_send.at[at, 0:2, 0:ROWS], x_recv.at[at, 1], x_ssem.at[at, 1],
                      x_rsem.at[at, 1], (g, lax.rem(b + boxes - 1, boxes)))
        pl.when(b < boxes - 1)(up.start)
        pl.when(b > 0)(down.start)
        flat = jnp.concatenate(d, axis=1)
        side_messages(flat, at)
        plane_copies = [
            remote(plane_send.at[at, k - 1], plane_recv.at[at, k - 1], plane_ssem.at[at, k - 1],
                   plane_rsem.at[at, k - 1], grp_peer(k))
            for k in range(1, groups)
        ]
        for copy in plane_copies:
            copy.start()

        def finish():
            d_high, d_low = split(flat, 2)
            d_cat = jnp.concatenate([d_high, d_high, d_low, jnp.zeros_like(d_low)], axis=0)
            progress = rate[...] * dot(order_parts, d_cat)
            q_high, q_low = split(progress, 2)
            both = dot(stoich_cat[...], q_high)
            chemistry = both[0:SP] + both[SP:] + dot(stoich_cat[0:SP, :], q_low)
            inner = jnp.concatenate(inner_sum(d), axis=1)
            image = flat + diffuse * (6.0 * flat - inner) - chemistry
            pl.when(b > 0)(up.wait_recv)
            pl.when(b < boxes - 1)(down.wait_recv)
            zero = jnp.zeros((ROWS, LANES), F32)
            outer = [padded(jnp.where(b > 0, x_recv[at, 0, ct], zero)) for ct in range(2)]
            outer += [
                padded(jnp.where(b < boxes - 1, x_recv[at, 1, ct], zero)) for ct in range(2)
            ]
            for copy in plane_copies:
                copy.wait_recv()
            image = image - diffuse * (jnp.concatenate(outer, axis=1) + side_ghosts(at))
            pl.when(b < boxes - 1)(up.wait_send)
            pl.when(b > 0)(down.wait_send)
            for copy in plane_copies:
                copy.wait_send()
            return image

        return flat, finish

    for copy in ghost_copies:
        copy.wait_send()

    direct[0], finish = send_halo(basis[0], 0)
    images[0] = finish()
    squares = []
    lengths = []
    columns = []
    for j in range(ITERS):
        more = j + 1 < ITERS
        image = images[j]
        known = [basis[i] for i in range(j + 1)]
        rows = [row_of(known[j], known[j])] + [row_of(v, image) for v in known]
        box_sums = reduce_rows(rows, j)
        if more:
            ahead, finish = send_halo(image, j + 1)
        all_sums = reduce_stage(box_sums(), j, 1)
        if more:
            ahead_image = finish()
        sums = sums_of(all_sums())
        sums = [sums[i : i + 1] for i in range(j + 2)]
        squares.append(sums[0])
        lengths.append(jnp.sqrt(sums[0]))
        columns.append([sums[1 + i] / (lengths[i] * lengths[j]) for i in range(j + 1)])
        parts = [sums[1 + i] / (squares[i] * lengths[j]) for i in range(j + 1)]
        scale = 1.0 / lengths[j]

        def corrected(field, past):
            field = field * scale
            for i in range(j + 1):
                field = field - parts[i] * past[i]
            return field

        basis[j + 1] = corrected(image, known)
        if more:
            direct[j + 1] = corrected(ahead, [direct[i] for i in range(j + 1)])
            images[j + 1] = corrected(ahead_image, [images[i] for i in range(j + 1)])

    last = basis[ITERS]
    box_sums = reduce_rows([row_of(last, last)], ITERS)
    for j in range(ITERS - 1):
        columns[j].append(lengths[j + 1])
    upper, target, ending = rotated(columns, lengths[0])
    none = jnp.zeros_like(lengths[0])
    fixed = back_substitute(upper, target, none)
    slope = back_substitute(upper, [none] * ITERS, none + 1.0)
    means = []
    cell = iota((256, LANES), 0)
    slot = iota((256, LANES), 1) & 63
    to_slot = (((((cell >> 7) << 3) + ((cell & 127) >> 4)) >> 1) << 3) + ((cell & 15) >> 1)
    for solved in (fixed, slope):
        total = sum((solved[j] / lengths[j]) * direct[j] for j in range(ITERS))
        means.append(total[:, 0:256] + total[:, 256:512])
    mean = exact_dot(jnp.concatenate(means, axis=0), ones_where(to_slot == slot), 3) * 0.125
    left = iota((ROWS, LANES), 1) < 64
    mean_send[...] = jnp.where(left, mean[0:ROWS], mean[SP : SP + ROWS])
    all_sums = reduce_stage(box_sums(), ITERS, 1)
    mean_copies = [
        remote(mean_send, mean_recv.at[k - 1], mean_ssem.at[k - 1], mean_rsem.at[k - 1], grp_peer(k))
        for k in range(1, groups)
    ]
    for copy in mean_copies:
        copy.start()
    length = jnp.sqrt(sums_of(all_sums())[0:1])
    radius = jnp.sqrt(ending * ending + length * length)
    final = (ending / radius) * target[ITERS - 1] / radius
    weights = back_substitute(upper, target, final)
    total = sum((weights[j] / lengths[j]) * direct[j] for j in range(ITERS))
    for x in range(2):
        for ct in range(2):
            k = 2 * x + ct
            flow[pl.ds(2 * ct + x, species, stride=4), :] = total[
                0:species, k * LANES : (k + 1) * LANES
            ]
    flow_copy = pltpu.make_async_copy(
        flow, correction_out.reshape(4 * species, LANES), load_sem.at[0]
    )
    flow_copy.start()
    for copy in mean_copies:
        copy.wait_recv()
    stage[...] = jnp.zeros_like(stage)
    stage[0:species, 0:256] = coarse_raw[...]
    blocks = [stage[0:ROWS, c * LANES : (c + 1) * LANES] for c in range(2)]
    for k in range(groups):
        message = mean_send[...] if k == 0 else mean_recv[k - 1]
        turned = pltpu.roll(message, 64, 1)
        message = jnp.where(left, message + final * turned, turned + final * message)
        for c in range(2):
            entry = average_list[0, lax.rem(g + groups - k, groups)] - (4 * g + 2 * c)
            blocks[c] = jnp.where(
                (left & (entry == 0)) | (~left & (entry == 1)), message, blocks[c]
            )
    for c in range(2):
        patch_new[:, c * LANES : (c + 1) * LANES] = blocks[c][0:species]
    patch_copy = pltpu.make_async_copy(patch_new, coarse_out.at[:, 0, :], load_sem.at[1])
    patch_copy.start()
    for copy in mean_copies:
        copy.wait_send()
    flow_copy.wait()
    patch_copy.wait()


def on_device(
    groups, boxes,
    source_term, diffusion, stoich, orders, rates, precond, coarse_field,
    neighbours, ghost_list, average_list,
):
    species = source_term.shape[0]
    reactions = rates.shape[0]

    def rows_of(x):
        lead = x.shape[:-3]
        x = x.reshape(lead + (2, 2, LANES))
        n = len(lead)
        x = x.transpose(tuple(range(n)) + (n + 1, n, n + 2))
        return x.reshape(-1, 2, LANES)

    hbm = pl.BlockSpec(memory_space=pl.ANY)
    smem = pl.BlockSpec(memory_space=pltpu.SMEM)
    count = 4 * species * species
    dma = pltpu.SemaphoreType.DMA
    reds = groups + boxes - 2
    correction, updated = pl.pallas_call(
        functools.partial(kernel, groups, boxes, species, reactions),
        out_shape=(
            jax.ShapeDtypeStruct((2 * species, 2, LANES), F32),
            jax.ShapeDtypeStruct((species, 1, 256), F32),
        ),
        in_specs=[smem, smem] + [hbm] * 8,
        out_specs=(hbm, hbm),
        scratch_shapes=[
            pltpu.VMEM((count, LANES), BF16),
            pltpu.VMEM((count + 4, LANES), F32),
            pltpu.VMEM((224, LANES), F32),
            pltpu.VMEM((232, LANES), F32),
            pltpu.VMEM((224, LANES), F32),
            pltpu.VMEM((ITERS, SP, 512), F32),
            pltpu.VMEM((ITERS, SP, 512), F32),
            pltpu.VMEM((ITERS + 1, SP, 512), F32),
            pltpu.VMEM((RP, 512), F32),
            pltpu.VMEM((SP, 512), F32),
            pltpu.VMEM((LANES, RP), F32),
            pltpu.VMEM((2 * SP, RP), BF16),
            pltpu.VMEM((512, LANES), BF16),
            pltpu.VMEM((LANES, 512), BF16),
            pltpu.VMEM((groups, 160), jnp.int32),
            pltpu.VMEM((groups, LANES), jnp.int32),
            pltpu.VMEM((4 * species, LANES), F32),
            pltpu.VMEM((1, species), F32),
            pltpu.VMEM((species, reactions), F32),
            pltpu.VMEM((species, reactions), F32),
            pltpu.VMEM((4 * reactions, LANES), F32),
            pltpu.VMEM((species, 256), F32),
            pltpu.VMEM((4 * species, LANES), F32),
            pltpu.VMEM((species, 256), F32),
            pltpu.VMEM((2, 4, SP, LANES), F32),
            pltpu.VMEM((groups - 1, ROWS, LANES), F32),
            pltpu.VMEM((groups - 1, ROWS, LANES), F32),
            pltpu.VMEM((2, groups - 1, 16, LANES), F32),
            pltpu.VMEM((2, groups - 1, 16, LANES), F32),
            pltpu.VMEM((2, 2, 2, ROWS, LANES), F32),
            pltpu.VMEM((2, 2, 8, LANES), F32),
            pltpu.VMEM((2, reds, 8, LANES), F32),
            pltpu.VMEM((ROWS, LANES), F32),
            pltpu.VMEM((groups - 1, ROWS, LANES), F32),
            dma((8,)),
            dma((groups - 1,)),
            dma((groups - 1,)),
            dma((2, groups - 1)),
            dma((2, groups - 1)),
            dma((2, 2)),
            dma((2, 2)),
            dma((2, reds)),
            dma((2, reds)),
            dma((groups - 1,)),
            dma((groups - 1,)),
        ],
        compiler_params=pltpu.CompilerParams(
            collective_id=0, has_side_effects=True, vmem_limit_bytes=63 * 1024 * 1024
        ),
        name="gmres",
    )(
        neighbours.T,
        average_list.T,
        ghost_list,
        rows_of(source_term),
        diffusion.reshape(1, species),
        stoich,
        orders.T,
        rows_of(rates),
        coarse_field,
        rows_of(precond),
    )
    correction = correction.reshape(species, 2, 2, LANES).transpose(0, 2, 1, 3)
    return (correction.reshape(species, 1, 2, 256), updated)


def solution(mesh):
    placed = (
        P(None, "grp", "box", None),
        P(),
        P(),
        P(),
        P(None, "grp", "box", None),
        P(None, None, "grp", "box", None),
        P(None, "grp", "box"),
        P(),
        P(None, "box", None),
        P(None, "box"),
    )
    return jax.shard_map(
        functools.partial(on_device, mesh.shape["grp"], mesh.shape["box"]),
        mesh=mesh,
        in_specs=placed,
        out_specs=(P(None, "grp", "box", None), P(None, "grp", "box")),
        check_vma=False,
    )
```

```python
import functools

import jax
import jax.numpy as jnp
from jax import lax
from jax.experimental import pallas as pl
from jax.experimental.pallas import tpu as pltpu
from jax.sharding import PartitionSpec as P

ITERS = 4
SP = 64
ROWS = 56
RP = 384
LANES = 128
MESH = pl.DeviceIdType.MESH
F32 = jnp.float32
BF16 = jnp.bfloat16


def least_squares(columns, beta):
    count = len(columns)
    target = [beta] + [jnp.zeros_like(beta)] * count
    rotations = []
    upper = []
    for j in range(count):
        entries = list(columns[j])
        for i in range(j):
            cosine_part, sine_part = rotations[i]
            first = cosine_part * entries[i] + sine_part * entries[i + 1]
            second = cosine_part * entries[i + 1] - sine_part * entries[i]
            entries[i] = first
            entries[i + 1] = second
        radius = jnp.sqrt(entries[j] * entries[j] + entries[j + 1] * entries[j + 1])
        cosine_part = entries[j] / radius
        sine_part = entries[j + 1] / radius
        rotations.append((cosine_part, sine_part))
        entries[j] = radius
        target[j + 1] = -sine_part * target[j]
        target[j] = cosine_part * target[j]
        upper.append(entries[: j + 1])
    result = [None] * count
    for j in reversed(range(count)):
        running = target[j]
        for k in range(j + 1, count):
            running = running - upper[k][j] * result[k]
        result[j] = running / upper[j][j]
    return result


def split(x, parts):
    pieces = []
    for _ in range(parts - 1):
        piece = x.astype(BF16)
        pieces.append(piece)
        x = x - piece.astype(F32)
    pieces.append(x.astype(BF16))
    return pieces


def dot(a, b):
    return jnp.dot(a, b, preferred_element_type=F32)


def exact_dot(x, ones, parts):
    rows = x.shape[0]
    product = dot(jnp.concatenate(split(x, parts), axis=0), ones)
    return sum(product[i * rows : (i + 1) * rows] for i in range(parts))


def iota(shape, dim):
    return lax.broadcasted_iota(jnp.int32, shape, dim)


def cell_of(index):
    k, l = index >> 7, index & 127
    return k >> 1, ((k & 1) << 3) + (l >> 4), l & 15


def on_face(face, t, y, z):
    return (
        ((face == 0) & (y == 0) & (z == t))
        | ((face == 1) & (y == 15) & (z == t))
        | ((face == 2) & (z == 0) & (y == t))
        | ((face == 3) & (z == 15) & (y == t))
    )


def ones_where(condition):
    return jnp.where(condition, 1.0, 0.0).astype(BF16)


def padded(x):
    return jnp.concatenate([x, jnp.zeros((SP - x.shape[0], x.shape[1]), F32)], axis=0)


def fields(x):
    return [x[:, k * LANES : (k + 1) * LANES] for k in range(4)]


def kernel(
    groups, boxes, species, reactions,
    neighbours, average_list, ghost_list, source, diffusion, stoich, orders, rates, coarse, precond,
    correction_out, coarse_out,
    raw, wide, even, odd, applied, direct, images, basis, rate, stage, tall, stoich_cat, pick, spread,
    lists, wanted_cells, source_raw, diffusion_raw, stoich_raw, orders_raw, rates_raw, coarse_raw,
    x_send, ghost_send, ghost_recv, plane_send, plane_recv, x_recv, red_send, red_recv,
    mean_send, mean_recv,
    load_sem, ghost_ssem, ghost_rsem, plane_ssem, plane_rsem, x_ssem, x_rsem,
    red_ssem, red_rsem, mean_ssem, mean_rsem,
):
    g = lax.axis_index("grp")
    b = lax.axis_index("box")
    barrier = pltpu.get_barrier_semaphore()

    def grp_peer(k):
        return (lax.rem(g + k, groups), b)

    def box_peer(k):
        return (g, lax.rem(b + k, boxes))

    for k in range(1, groups):
        pl.semaphore_signal(barrier, inc=1, device_id=grp_peer(k), device_id_type=MESH)
    for k in range(1, boxes):
        pl.semaphore_signal(barrier, inc=1, device_id=box_peer(k), device_id_type=MESH)

    def remote(src, dst, ssem, rsem, device):
        return pltpu.make_async_remote_copy(
            src_ref=src, dst_ref=dst, send_sem=ssem, recv_sem=rsem,
            device_id=device, device_id_type=MESH,
        )

    loads = [
        pltpu.make_async_copy(src, dst, load_sem.at[i])
        for i, (src, dst) in enumerate((
            (ghost_list.at[:, 0, :], lists),
            (coarse.at[:, 0, :], coarse_raw),
            (precond.reshape(4 * species * species, LANES), raw),
            (rates.reshape(4 * reactions, LANES), rates_raw),
            (orders, orders_raw),
            (stoich, stoich_raw),
            (diffusion, diffusion_raw),
            (source.reshape(4 * species, LANES), source_raw),
        ))
    ]
    for load in loads:
        load.start()

    stage[...] = jnp.zeros_like(stage)
    loads[0].wait()
    loads[1].wait()
    stage[0:species, 0:256] = coarse_raw[...]
    x_slots = lists[:, 0:LANES]
    x_slots = jnp.where(b == 0, x_slots, pltpu.roll(x_slots, 64, 1))
    side_slots = jnp.concatenate(
        [
            jnp.full((groups, 64), -1, jnp.int32),
            lists[:, LANES : LANES + 32],
            jnp.full((groups, 32), -1, jnp.int32),
        ],
        axis=1,
    )
    wanted_cells[...] = jnp.where(iota((groups, LANES), 1) < 64, x_slots, side_slots)
    patch = jnp.concatenate(split(stage[:, 0:256], 3), axis=0)
    cell = iota((256, LANES), 0) + g * 256

    at_end = (b == 0) | (b == boxes - 1)
    short = iota((16, LANES), 1)
    left = iota((32, LANES), 1) < 64

    def chosen(k):
        wanted = wanted_cells[pl.ds(lax.rem(g + k, groups), 1), :]
        got = dot(patch, ones_where(cell == wanted))
        got = got[0:SP] + got[SP : 2 * SP] + got[2 * SP :]
        side_part = got[0:16]
        side_part = pltpu.roll(side_part, 64, 1)
        for q in range(1, 4):
            rows = got[16 * q : 16 * q + 16]
            rows = rows if q == 2 else pltpu.roll(rows, (32 * q - 64) % LANES, 1)
            side_part = jnp.where((short >> 5) == q, rows, side_part)
        x_part = jnp.where(left, got[0:32], pltpu.roll(got[32:64], 64, 1))
        return jnp.concatenate([side_part, x_part], axis=0)

    for k in range(1, groups):
        ghost_send[k - 1] = chosen(k)
    own_ghosts = chosen(0)
    pl.semaphore_wait(barrier, groups + boxes - 2)

    def ghost_copies(rows):
        return [
            remote(ghost_send.at[k - 1, 0:rows], ghost_recv.at[k - 1, 0:rows],
                   ghost_ssem.at[k - 1], ghost_rsem.at[k - 1], grp_peer(k))
            for k in range(1, groups)
        ]

    def for_ghosts(act):
        @pl.when(at_end)
        def _():
            for copy in ghost_copies(48):
                act(copy)

        @pl.when(jnp.logical_not(at_end))
        def _():
            for copy in ghost_copies(16):
                act(copy)

    for_ghosts(lambda copy: copy.start())

    even[...] = jnp.zeros_like(even)
    odd[...] = jnp.zeros_like(odd)
    applied[...] = jnp.zeros_like(applied)
    rate[...] = jnp.zeros_like(rate)
    for load in loads[3:]:
        load.wait()
    for x in range(2):
        for ct in range(2):
            k = 2 * x + ct
            rate[0:reactions, k * LANES : (k + 1) * LANES] = rates_raw[
                pl.ds(2 * ct + x, reactions, stride=4), :
            ]
    tall[...] = jnp.zeros_like(tall)
    tall[0:species, 0:reactions] = orders_raw[...]
    whole = tall[...].T
    high = whole.astype(BF16).astype(F32)
    low = whole - high
    order_parts = jnp.concatenate([high + pltpu.roll(low, 64, 1), high], axis=1).astype(BF16)
    stage[...] = jnp.zeros_like(stage)
    stage[0:species, 0:reactions] = stoich_raw[...]
    whole = stage[:, 0:RP]
    stoich_high, stoich_low = split(whole, 2)
    stoich_cat[0:SP, :] = stoich_high
    stoich_cat[SP : 2 * SP, :] = stoich_low
    x, y, z = cell_of(iota((512, LANES), 0))
    slot = iota((512, LANES), 1)
    pick[...] = ones_where(((slot >> 4 & 1) == x) & on_face(slot >> 5, slot & 15, y, z))
    x, y, z = cell_of(iota((LANES, 512), 1))
    slot = iota((LANES, 512), 0)
    spread[...] = ones_where(((slot >> 4 & 1) == x) & on_face(slot >> 5, slot & 15, y, z))
    end = jnp.where(b == 0, 0, 1)
    behind_x = (slot < 64) & (x == end) & (((y >> 1) << 3) + (z >> 1) == slot)
    past = slot - 64
    face = past >> 3
    t = jnp.where(face < 2, z, y)
    behind_side = (slot >= 64) & (slot < 96) & ((t >> 1) == (past & 7)) & on_face(face, t, y, z)
    coarse_spread = ones_where(behind_x | behind_side)

    loads[2].wait()
    count = species * species * 4
    chunk = 432
    steps = count // chunk

    def widen(i, carry):
        at = pl.multiple_of(i * chunk, 16)
        wide[pl.ds(at, chunk), :] = raw[pl.ds(at, chunk), :].astype(F32)
        return carry

    lax.fori_loop(0, steps, widen, 0)
    tail = steps * chunk
    wide[tail:, :] = jnp.zeros((wide.shape[0] - tail, LANES), F32)
    wide[tail:count, :] = raw[tail:count, :].astype(F32)

    tall[0:8, 0:LANES] = jnp.zeros((8, LANES), F32)
    tall[0:1, 0:species] = diffusion_raw[...]
    same = iota((SP, LANES), 0) == iota((SP, LANES), 1)
    diffuse = jnp.sum(jnp.where(same, tall[0:1, 0:LANES], 0.0), axis=1, keepdims=True)
    diffuse = jnp.broadcast_to(diffuse, (SP, 512))
    stage[...] = jnp.zeros_like(stage)
    for x in range(2):
        for ct in range(2):
            k = 2 * x + ct
            stage[0:species, k * LANES : (k + 1) * LANES] = source_raw[
                pl.ds(2 * ct + x, species, stride=4), :
            ]
    for_ghosts(lambda copy: copy.wait_recv())
    side_part = own_ghosts[0:16]
    x_part = jnp.where(at_end, own_ghosts[16:48], 0.0)
    for k in range(1, groups):
        side_part = side_part + ghost_recv[k - 1, 0:16]
        x_part = x_part + jnp.where(at_end, ghost_recv[k - 1, 16:48], 0.0)
    side_part = jnp.concatenate(
        [
            pltpu.roll(side_part, 64, 1),
            pltpu.roll(side_part, 32, 1),
            side_part,
            pltpu.roll(side_part, 96, 1),
        ],
        axis=0,
    )
    x_part = jnp.concatenate([x_part, pltpu.roll(x_part, 64, 1)], axis=0)
    place = iota((SP, LANES), 1)
    values = jnp.where(place < 64, x_part, jnp.where(place < 96, side_part, 0.0))
    basis[0] = stage[...] + diffuse * exact_dot(values, coarse_spread, 3)

    half = species // 2

    def apply_inverse(v):
        for x in range(2):
            for ct in range(2):
                part = v[0:ROWS, (2 * x + ct) * LANES : (2 * x + ct + 1) * LANES]
                even[pl.ds(2 * ct + x, ROWS, stride=4), :] = part
                odd[pl.ds(4 + 2 * ct + x, ROWS, stride=4), :] = part
        rows = 4 * species + 4
        low_half = iota((8, LANES), 0) < 4

        def product(at, vector):
            p = (wide[pl.ds(pl.multiple_of(at, 8), rows), :] * vector).reshape(
                rows // 8, 8, LANES
            )
            parts = [p[i] for i in range(rows // 8)]
            while len(parts) > 1:
                pairs = [a + c for a, c in zip(parts[0::2], parts[1::2])]
                parts = pairs + ([parts[-1]] if len(parts) % 2 else [])
            return parts[0] + pltpu.roll(parts[0], 4, 0)

        def sweep(count, start, vector, store):
            def step(m, carry):
                store(m, product(m * (8 * species) + start, vector))
                return carry

            def four(m, carry):
                for i in range(4):
                    step(4 * m + i, carry)
                return carry

            lax.fori_loop(0, count // 4, four, 0)
            for m in range(count // 4 * 4, count):
                step(m, 0)

        def store_even(m, value):
            applied[pl.ds(pl.multiple_of(m * 8, 8), 8), :] = value

        def store_odd(m, value):
            at = pl.ds(pl.multiple_of(m * 8, 8), 8)
            applied[at, :] = jnp.where(low_half, applied[at, :], value)

        sweep(half + 1, 0, even[0:rows, :], store_even)
        sweep(half, 4 * species - 4, odd[0:rows, :], store_odd)
        tail_at = pl.ds(8 * half, 8)
        applied[tail_at, :] = jnp.where(low_half, applied[tail_at, :], 0.0)
        return [
            padded(applied[pl.ds(2 * ct + x, ROWS, stride=4), :])
            for x in range(2)
            for ct in range(2)
        ]

    lane = iota((16, LANES), 1)
    wide_lane = iota((SP, LANES), 1)
    links = [neighbours[f, g] for f in range(4)]

    def rolled(x, shift):
        shift = shift % LANES
        return pltpu.roll(x, shift, 1) if shift else x

    def side_messages(flat, at):
        planes = exact_dot(flat, pick[...], 2)
        packed = []
        for f in range(4):
            total = jnp.zeros((16, LANES), F32)
            for q in range(4):
                rows = planes[16 * q : 16 * q + 16]
                total = jnp.where((lane >> 5) == q, rolled(rows, 32 * (q - f)), total)
            packed.append(total)
        for k in range(1, groups):
            peer = lax.rem(g + k, groups)
            message = jnp.zeros((16, LANES), F32)
            for f in range(4):
                message = jnp.where(links[f] == peer, packed[f], message)
            plane_send[at, k - 1] = message

    def side_ghosts(at):
        found = [jnp.zeros((16, LANES), F32)] * 4
        for k in range(1, groups):
            peer = lax.rem(g + groups - k, groups)
            message = plane_recv[at, k - 1]
            found = [
                jnp.where(links[f] == peer, message, found[f]) for f in range(4)
            ]
        rows = []
        for q in range(4):
            total = jnp.zeros((16, LANES), F32)
            for f in range(4):
                total = jnp.where((lane >> 5) == f, rolled(found[f], 32 * (f - q)), total)
            rows.append(total)
        return exact_dot(jnp.concatenate(rows, axis=0), spread[...], 2)

    def inner_sum(d):
        result = []
        zero = jnp.zeros((SP, LANES), F32)
        z = wide_lane & 15
        for x in range(2):
            plane = d[2 * x : 2 * x + 2]
            up = [rolled(p, -16) for p in plane]
            down = [rolled(p, 16) for p in plane]
            for ct in range(2):
                own = plane[ct]
                total = d[2 * (1 - x) + ct]
                total = total + jnp.where(z == 15, 0.0, rolled(own, -1))
                total = total + jnp.where(z == 0, 0.0, rolled(own, 1))
                total = total + jnp.where(wide_lane >= 112, up[1] if ct == 0 else zero, up[ct])
                total = total + jnp.where(wide_lane < 16, down[0] if ct == 1 else zero, down[ct])
                result.append(total)
        return result

    def row_of(a, c):
        p = a * c
        p = p[:, 0:128] + p[:, 128:256] + p[:, 256:384] + p[:, 384:512]
        return jnp.sum(p, axis=0, keepdims=True)

    def reduce_stage(tile, turn, stage_id):
        at = turn % 2
        first, size, peer = ((0, boxes, box_peer), (boxes - 1, groups, grp_peer))[stage_id]
        high = tile.shape[0]
        red_send[at, stage_id, 0:high] = tile
        copies = [
            remote(red_send.at[at, stage_id, 0:high], red_recv.at[at, first + k - 1, 0:high],
                   red_ssem.at[at, first + k - 1], red_rsem.at[at, first + k - 1], peer(k))
            for k in range(1, size)
        ]
        for copy in copies:
            copy.start()

        def finish():
            total = tile
            for copy in copies:
                copy.wait_recv()
            for k in range(1, size):
                total = total + red_recv[at, first + k - 1, 0:high]
            for copy in copies:
                copy.wait_send()
            return total

        return finish

    def reduce_rows(rows, turn):
        high = -(-len(rows) // 8) * 8
        row_id = iota((high, LANES), 0)
        tile = jnp.zeros((high, LANES), F32)
        for i, row in enumerate(rows):
            tile = jnp.where(row_id == i, row, tile)
        return reduce_stage(tile, turn, 0)

    def sums_of(tile):
        return jnp.sum(tile, axis=1, keepdims=True)

    def send_halo(v, turn):
        at = turn % 2
        d = apply_inverse(v)
        for k in range(4):
            x_send[at, k] = d[k]
        up = remote(x_send.at[at, 2:4, 0:ROWS], x_recv.at[at, 0], x_ssem.at[at, 0],
                    x_rsem.at[at, 0], (g, lax.rem(b + 1, boxes)))
        down = remote(x_send.at[at, 0:2, 0:ROWS], x_recv.at[at, 1], x_ssem.at[at, 1],
                      x_rsem.at[at, 1], (g, lax.rem(b + boxes - 1, boxes)))
        pl.when(b < boxes - 1)(up.start)
        pl.when(b > 0)(down.start)
        flat = jnp.concatenate(d, axis=1)
        side_messages(flat, at)
        plane_copies = [
            remote(plane_send.at[at, k - 1], plane_recv.at[at, k - 1], plane_ssem.at[at, k - 1],
                   plane_rsem.at[at, k - 1], grp_peer(k))
            for k in range(1, groups)
        ]
        for copy in plane_copies:
            copy.start()

        def finish():
            d_high, d_low = split(flat, 2)
            d_cat = jnp.concatenate([d_high, d_high, d_low, jnp.zeros_like(d_low)], axis=0)
            progress = rate[...] * dot(order_parts, d_cat)
            q_high, q_low = split(progress, 2)
            both = dot(stoich_cat[...], q_high)
            chemistry = both[0:SP] + both[SP:] + dot(stoich_cat[0:SP, :], q_low)
            inner = jnp.concatenate(inner_sum(d), axis=1)
            image = flat + diffuse * (6.0 * flat - inner) - chemistry
            pl.when(b > 0)(up.wait_recv)
            pl.when(b < boxes - 1)(down.wait_recv)
            zero = jnp.zeros((ROWS, LANES), F32)
            outer = [padded(jnp.where(b > 0, x_recv[at, 0, ct], zero)) for ct in range(2)]
            outer += [
                padded(jnp.where(b < boxes - 1, x_recv[at, 1, ct], zero)) for ct in range(2)
            ]
            for copy in plane_copies:
                copy.wait_recv()
            image = image - diffuse * (jnp.concatenate(outer, axis=1) + side_ghosts(at))
            pl.when(b < boxes - 1)(up.wait_send)
            pl.when(b > 0)(down.wait_send)
            for copy in plane_copies:
                copy.wait_send()
            return image

        return flat, finish

    for_ghosts(lambda copy: copy.wait_send())

    direct[0], finish = send_halo(basis[0], 0)
    images[0] = finish()
    gram = {}
    squares = []
    lengths = []
    columns = []
    for j in range(ITERS):
        more = j + 1 < ITERS
        image = images[j]
        known = [basis[i] for i in range(j + 1)]
        rows = [row_of(known[j], known[j])] + [row_of(v, image) for v in known]
        rows += [row_of(v, known[j]) for v in known[:j]]
        if not more:
            rows.append(row_of(image, image))
        box_sums = reduce_rows(rows, j)
        if more:
            ahead, finish = send_halo(image, j + 1)
        all_sums = reduce_stage(box_sums(), j, 1)
        if more:
            ahead_image = finish()
        else:
            cell = iota((256, LANES), 0)
            slot = iota((256, LANES), 1) & 63
            to_slot = ((((cell >> 7) << 3) + ((cell & 127) >> 4)) >> 1) << 3
            to_slot = ones_where(to_slot + ((cell & 15) >> 1) == slot)
            means = []
            for i in range(ITERS):
                folded = direct[i, :, 0:256] + direct[i, :, 256:512]
                mean = exact_dot(folded, to_slot, 3) * 0.125
                means.append(jnp.where(left, mean[0:32], mean[32:64]))
        sums = sums_of(all_sums())
        sums = [sums[i : i + 1] for i in range(len(rows))]
        squares.append(sums[0])
        lengths.append(jnp.sqrt(sums[0]))
        columns.append([sums[1 + i] / (lengths[i] * lengths[j]) for i in range(j + 1)])
        for i in range(j):
            gram[i, j] = sums[j + 2 + i]
        parts = [sums[1 + i] / (squares[i] * lengths[j]) for i in range(j + 1)]
        scale = 1.0 / lengths[j]

        def corrected(field, past):
            field = field * scale
            for i in range(j + 1):
                field = field - parts[i] * past[i]
            return field

        if more:
            basis[j + 1] = corrected(image, known)
            direct[j + 1] = corrected(ahead, [direct[i] for i in range(j + 1)])
            images[j + 1] = corrected(ahead_image, [images[i] for i in range(j + 1)])

    ratios = [sums[1 + i] / squares[i] for i in range(ITERS)]
    square = sums[-1]
    for i in range(ITERS):
        square = square - ratios[i] * sums[1 + i]
    for (i, k), entry in gram.items():
        square = square + 2.0 * ratios[i] * ratios[k] * entry
    length = jnp.sqrt(jnp.maximum(square, 0.0)) / lengths[ITERS - 1]
    for j in range(ITERS):
        columns[j].append((lengths + [length])[j + 1])
    weights = least_squares(columns, lengths[0])
    scales = [weights[j] / lengths[j] for j in range(ITERS)]
    mean_send[...] = sum(scales[j] * means[j] for j in range(ITERS))
    mean_copies = [
        remote(mean_send, mean_recv.at[k - 1], mean_ssem.at[k - 1], mean_rsem.at[k - 1], grp_peer(k))
        for k in range(1, groups)
    ]
    for copy in mean_copies:
        copy.start()
    total = sum(scales[j] * direct[j] for j in range(ITERS))
    for x in range(2):
        for ct in range(2):
            k = 2 * x + ct
            correction_out[pl.ds(ct, species, stride=2), x, :] = total[
                0:species, k * LANES : (k + 1) * LANES
            ]
    stage[...] = jnp.zeros_like(stage)
    stage[0:species, 0:256] = coarse_raw[...]
    blocks = [stage[:, c * LANES : (c + 1) * LANES] for c in range(2)]
    for copy in mean_copies:
        copy.wait_recv()
    left_half = iota((SP, LANES), 1) < 64
    for k in range(groups):
        message = mean_send[...] if k == 0 else mean_recv[k - 1]
        turned = pltpu.roll(message, 64, 1)
        message = jnp.concatenate(
            [jnp.where(left, message, turned), jnp.where(left, turned, message)], axis=0
        )
        for c in range(2):
            entry = average_list[0, lax.rem(g + groups - k, groups)] - (4 * g + 2 * c)
            blocks[c] = jnp.where(
                (left_half & (entry == 0)) | (~left_half & (entry == 1)), message, blocks[c]
            )
    for c in range(2):
        coarse_out[:, 0, c * LANES : (c + 1) * LANES] = blocks[c][0:species]
    for copy in mean_copies:
        copy.wait_send()


def on_device(
    groups, boxes,
    source_term, diffusion, stoich, orders, rates, precond, coarse_field,
    neighbours, ghost_list, average_list,
):
    species = source_term.shape[0]
    reactions = rates.shape[0]

    def rows_of(x):
        lead = x.shape[:-3]
        x = x.reshape(lead + (2, 2, LANES))
        n = len(lead)
        x = x.transpose(tuple(range(n)) + (n + 1, n, n + 2))
        return x.reshape(-1, 2, LANES)

    hbm = pl.BlockSpec(memory_space=pl.ANY)
    smem = pl.BlockSpec(memory_space=pltpu.SMEM)
    count = 4 * species * species
    dma = pltpu.SemaphoreType.DMA
    reds = groups + boxes - 2
    correction, updated = pl.pallas_call(
        functools.partial(kernel, groups, boxes, species, reactions),
        out_shape=(
            jax.ShapeDtypeStruct((2 * species, 2, LANES), F32),
            jax.ShapeDtypeStruct((species, 1, 256), F32),
        ),
        in_specs=[smem, smem] + [hbm] * 8,
        out_specs=(pl.BlockSpec(memory_space=pltpu.VMEM),) * 2,
        scratch_shapes=[
            pltpu.VMEM((count, LANES), BF16),
            pltpu.VMEM((count + 4, LANES), F32),
            pltpu.VMEM((224, LANES), F32),
            pltpu.VMEM((232, LANES), F32),
            pltpu.VMEM((224, LANES), F32),
            pltpu.VMEM((ITERS, SP, 512), F32),
            pltpu.VMEM((ITERS, SP, 512), F32),
            pltpu.VMEM((ITERS + 1, SP, 512), F32),
            pltpu.VMEM((RP, 512), F32),
            pltpu.VMEM((SP, 512), F32),
            pltpu.VMEM((LANES, RP), F32),
            pltpu.VMEM((2 * SP, RP), BF16),
            pltpu.VMEM((512, LANES), BF16),
            pltpu.VMEM((LANES, 512), BF16),
            pltpu.VMEM((groups, 160), jnp.int32),
            pltpu.VMEM((groups, LANES), jnp.int32),
            pltpu.VMEM((4 * species, LANES), F32),
            pltpu.VMEM((1, species), F32),
            pltpu.VMEM((species, reactions), F32),
            pltpu.VMEM((species, reactions), F32),
            pltpu.VMEM((4 * reactions, LANES), F32),
            pltpu.VMEM((species, 256), F32),
            pltpu.VMEM((2, 4, SP, LANES), F32),
            pltpu.VMEM((groups - 1, 48, LANES), F32),
            pltpu.VMEM((groups - 1, 48, LANES), F32),
            pltpu.VMEM((2, groups - 1, 16, LANES), F32),
            pltpu.VMEM((2, groups - 1, 16, LANES), F32),
            pltpu.VMEM((2, 2, 2, ROWS, LANES), F32),
            pltpu.VMEM((2, 2, 16, LANES), F32),
            pltpu.VMEM((2, reds, 16, LANES), F32),
            pltpu.VMEM((32, LANES), F32),
            pltpu.VMEM((groups - 1, 32, LANES), F32),
            dma((8,)),
            dma((groups - 1,)),
            dma((groups - 1,)),
            dma((2, groups - 1)),
            dma((2, groups - 1)),
            dma((2, 2)),
            dma((2, 2)),
            dma((2, reds)),
            dma((2, reds)),
            dma((groups - 1,)),
            dma((groups - 1,)),
        ],
        compiler_params=pltpu.CompilerParams(
            collective_id=0, has_side_effects=True, vmem_limit_bytes=63 * 1024 * 1024
        ),
        name="gmres",
    )(
        neighbours.T,
        average_list.T,
        ghost_list,
        rows_of(source_term),
        diffusion.reshape(1, species),
        stoich,
        orders.T,
        rows_of(rates),
        coarse_field,
        rows_of(precond),
    )
    correction = correction.reshape(species, 2, 2, LANES).transpose(0, 2, 1, 3)
    return (correction.reshape(species, 1, 2, 256), updated)


def solution(mesh):
    placed = (
        P(None, "grp", "box", None),
        P(),
        P(),
        P(),
        P(None, "grp", "box", None),
        P(None, None, "grp", "box", None),
        P(None, "grp", "box"),
        P(),
        P(None, "box", None),
        P(None, "box"),
    )
    return jax.shard_map(
        functools.partial(on_device, mesh.shape["grp"], mesh.shape["box"]),
        mesh=mesh,
        in_specs=placed,
        out_specs=(P(None, "grp", "box", None), P(None, "grp", "box")),
        check_vma=False,
    )
```

```python
import functools

import jax
import jax.numpy as jnp
from jax import lax
from jax.experimental import pallas as pl
from jax.experimental.pallas import tpu as pltpu
from jax.sharding import PartitionSpec as P

ITERS = 4
SP = 64
ROWS = 56
RP = 384
LANES = 128
MESH = pl.DeviceIdType.MESH
F32 = jnp.float32
BF16 = jnp.bfloat16


def least_squares(columns, beta):
    count = len(columns)
    target = [beta] + [jnp.zeros_like(beta)] * count
    rotations = []
    upper = []
    for j in range(count):
        entries = list(columns[j])
        for i in range(j):
            cosine_part, sine_part = rotations[i]
            first = cosine_part * entries[i] + sine_part * entries[i + 1]
            second = cosine_part * entries[i + 1] - sine_part * entries[i]
            entries[i] = first
            entries[i + 1] = second
        radius = jnp.sqrt(entries[j] * entries[j] + entries[j + 1] * entries[j + 1])
        cosine_part = entries[j] / radius
        sine_part = entries[j + 1] / radius
        rotations.append((cosine_part, sine_part))
        entries[j] = radius
        target[j + 1] = -sine_part * target[j]
        target[j] = cosine_part * target[j]
        upper.append(entries[: j + 1])
    result = [None] * count
    for j in reversed(range(count)):
        running = target[j]
        for k in range(j + 1, count):
            running = running - upper[k][j] * result[k]
        result[j] = running / upper[j][j]
    return result


def split(x, parts):
    pieces = []
    for _ in range(parts - 1):
        piece = x.astype(BF16)
        pieces.append(piece)
        x = x - piece.astype(F32)
    pieces.append(x.astype(BF16))
    return pieces


def dot(a, b):
    return jnp.dot(a, b, preferred_element_type=F32)


def exact_dot(x, ones, parts):
    rows = x.shape[0]
    product = dot(jnp.concatenate(split(x, parts), axis=0), ones)
    return sum(product[i * rows : (i + 1) * rows] for i in range(parts))


def iota(shape, dim):
    return lax.broadcasted_iota(jnp.int32, shape, dim)


def cell_of(index):
    k, l = index >> 7, index & 127
    return k >> 1, ((k & 1) << 3) + (l >> 4), l & 15


def on_face(face, t, y, z):
    return (
        ((face == 0) & (y == 0) & (z == t))
        | ((face == 1) & (y == 15) & (z == t))
        | ((face == 2) & (z == 0) & (y == t))
        | ((face == 3) & (z == 15) & (y == t))
    )


def ones_where(condition):
    return jnp.where(condition, 1.0, 0.0).astype(BF16)


def padded(x):
    return jnp.concatenate([x, jnp.zeros((SP - x.shape[0], x.shape[1]), F32)], axis=0)


def fields(x):
    return [x[:, k * LANES : (k + 1) * LANES] for k in range(4)]


def kernel(
    groups, boxes, species, reactions,
    neighbours, average_list, ghost_list, source, diffusion, stoich, orders, rates, coarse, precond,
    correction_out, coarse_out,
    raw, wide, even, odd, applied, direct, images, basis, rate, stage, tall, stoich_cat, pick, spread,
    lists, wanted_cells, source_raw, diffusion_raw, stoich_raw, orders_raw, rates_raw, coarse_raw,
    x_send, ghost_send, ghost_recv, plane_send, plane_recv, x_recv, red_send, red_recv,
    mean_send, mean_recv,
    load_sem, ghost_ssem, ghost_rsem, plane_ssem, plane_rsem, x_ssem, x_rsem,
    red_ssem, red_rsem, mean_ssem, mean_rsem,
):
    g = lax.axis_index("grp")
    b = lax.axis_index("box")
    barrier = pltpu.get_barrier_semaphore()

    def grp_peer(k):
        return (lax.rem(g + k, groups), b)

    def box_peer(k):
        return (g, lax.rem(b + k, boxes))

    for k in range(1, groups):
        pl.semaphore_signal(barrier, inc=1, device_id=grp_peer(k), device_id_type=MESH)
    for k in range(1, boxes):
        pl.semaphore_signal(barrier, inc=1, device_id=box_peer(k), device_id_type=MESH)

    def remote(src, dst, ssem, rsem, device):
        return pltpu.make_async_remote_copy(
            src_ref=src, dst_ref=dst, send_sem=ssem, recv_sem=rsem,
            device_id=device, device_id_type=MESH,
        )

    def wait_bytes(ref, sem):
        pltpu.make_async_copy(ref, ref, sem).wait()

    loads = [
        pltpu.make_async_copy(src, dst, load_sem.at[i])
        for i, (src, dst) in enumerate((
            (ghost_list.at[:, 0, :], lists),
            (coarse.at[:, 0, :], coarse_raw),
            (precond.reshape(4 * species * species, LANES), raw),
            (rates.reshape(4 * reactions, LANES), rates_raw),
            (orders, orders_raw),
            (stoich, stoich_raw),
            (diffusion, diffusion_raw),
            (source.reshape(4 * species, LANES), source_raw),
        ))
    ]
    for load in loads:
        load.start()

    stage[...] = jnp.zeros_like(stage)
    even[...] = jnp.zeros_like(even)
    odd[...] = jnp.zeros_like(odd)
    applied[...] = jnp.zeros_like(applied)
    rate[...] = jnp.zeros_like(rate)
    x, y, z = cell_of(iota((512, LANES), 0))
    slot = iota((512, LANES), 1)
    pick[...] = ones_where(((slot >> 4 & 1) == x) & on_face(slot >> 5, slot & 15, y, z))
    x, y, z = cell_of(iota((LANES, 512), 1))
    slot = iota((LANES, 512), 0)
    spread[...] = ones_where(((slot >> 4 & 1) == x) & on_face(slot >> 5, slot & 15, y, z))
    end = jnp.where(b == 0, 0, 1)
    behind_x = (slot < 64) & (x == end) & (((y >> 1) << 3) + (z >> 1) == slot)
    past = slot - 64
    face = past >> 3
    t = jnp.where(face < 2, z, y)
    behind_side = (slot >= 64) & (slot < 96) & ((t >> 1) == (past & 7)) & on_face(face, t, y, z)
    coarse_spread = ones_where(behind_x | behind_side)
    loads[0].wait()
    loads[1].wait()
    stage[0:species, 0:256] = coarse_raw[...]
    x_slots = lists[:, 0:LANES]
    x_slots = jnp.where(b == 0, x_slots, pltpu.roll(x_slots, 64, 1))
    side_slots = jnp.concatenate(
        [
            jnp.full((groups, 64), -1, jnp.int32),
            lists[:, LANES : LANES + 32],
            jnp.full((groups, 32), -1, jnp.int32),
        ],
        axis=1,
    )
    wanted_cells[...] = jnp.where(iota((groups, LANES), 1) < 64, x_slots, side_slots)
    patch = jnp.concatenate(split(stage[:, 0:256], 3), axis=0)
    cell = iota((256, LANES), 0) + g * 256

    at_end = (b == 0) | (b == boxes - 1)
    short = iota((16, LANES), 1)
    left = iota((32, LANES), 1) < 64

    def chosen(k):
        wanted = wanted_cells[pl.ds(lax.rem(g + k, groups), 1), :]
        got = dot(patch, ones_where(cell == wanted))
        got = got[0:SP] + got[SP : 2 * SP] + got[2 * SP :]
        side_part = got[0:16]
        side_part = pltpu.roll(side_part, 64, 1)
        for q in range(1, 4):
            rows = got[16 * q : 16 * q + 16]
            rows = rows if q == 2 else pltpu.roll(rows, (32 * q - 64) % LANES, 1)
            side_part = jnp.where((short >> 5) == q, rows, side_part)
        x_part = jnp.where(left, got[0:32], pltpu.roll(got[32:64], 64, 1))
        return jnp.concatenate([side_part, x_part], axis=0)

    for k in range(1, groups):
        ghost_send[k - 1] = chosen(k)
    pl.semaphore_wait(barrier, groups + boxes - 2)

    def ghost_copies(rows):
        return [
            remote(ghost_send.at[k - 1, 0:rows], ghost_recv.at[k - 1, 0:rows],
                   ghost_ssem, ghost_rsem, grp_peer(k))
            for k in range(1, groups)
        ]

    def start_ghosts(rows):
        for copy in ghost_copies(rows):
            copy.start()

    def wait_ghosts(ref, sem):
        pl.when(at_end)(lambda: wait_bytes(ref.at[:, 0:48], sem))
        pl.when(jnp.logical_not(at_end))(lambda: wait_bytes(ref.at[:, 0:16], sem))

    pl.when(at_end)(lambda: start_ghosts(48))
    pl.when(jnp.logical_not(at_end))(lambda: start_ghosts(16))
    own_ghosts = chosen(0)

    for load in loads[3:]:
        load.wait()
    for x in range(2):
        for ct in range(2):
            k = 2 * x + ct
            rate[0:reactions, k * LANES : (k + 1) * LANES] = rates_raw[
                pl.ds(2 * ct + x, reactions, stride=4), :
            ]
    tall[...] = jnp.zeros_like(tall)
    tall[0:species, 0:reactions] = orders_raw[...]
    whole = tall[...].T
    high = whole.astype(BF16).astype(F32)
    low = whole - high
    order_parts = jnp.concatenate([high + pltpu.roll(low, 64, 1), high], axis=1).astype(BF16)
    stage[...] = jnp.zeros_like(stage)
    stage[0:species, 0:reactions] = stoich_raw[...]
    whole = stage[:, 0:RP]
    stoich_high, stoich_low = split(whole, 2)
    stoich_cat[0:SP, :] = stoich_high
    stoich_cat[SP : 2 * SP, :] = stoich_low
    loads[2].wait()
    count = species * species * 4
    chunk = 432
    steps = count // chunk

    def widen(i, carry):
        at = pl.multiple_of(i * chunk, 16)
        wide[pl.ds(at, chunk), :] = raw[pl.ds(at, chunk), :].astype(F32)
        return carry

    lax.fori_loop(0, steps, widen, 0)
    tail = steps * chunk
    wide[tail:, :] = jnp.zeros((wide.shape[0] - tail, LANES), F32)
    wide[tail:count, :] = raw[tail:count, :].astype(F32)

    tall[0:8, 0:LANES] = jnp.zeros((8, LANES), F32)
    tall[0:1, 0:species] = diffusion_raw[...]
    same = iota((SP, LANES), 0) == iota((SP, LANES), 1)
    diffuse = jnp.sum(jnp.where(same, tall[0:1, 0:LANES], 0.0), axis=1, keepdims=True)
    diffuse = jnp.broadcast_to(diffuse, (SP, 512))
    stage[...] = jnp.zeros_like(stage)
    for x in range(2):
        for ct in range(2):
            k = 2 * x + ct
            stage[0:species, k * LANES : (k + 1) * LANES] = source_raw[
                pl.ds(2 * ct + x, species, stride=4), :
            ]
    wait_ghosts(ghost_recv, ghost_rsem)
    side_part = own_ghosts[0:16]
    x_part = jnp.where(at_end, own_ghosts[16:48], 0.0)
    for k in range(1, groups):
        side_part = side_part + ghost_recv[k - 1, 0:16]
        x_part = x_part + jnp.where(at_end, ghost_recv[k - 1, 16:48], 0.0)
    side_part = jnp.concatenate(
        [
            pltpu.roll(side_part, 64, 1),
            pltpu.roll(side_part, 32, 1),
            side_part,
            pltpu.roll(side_part, 96, 1),
        ],
        axis=0,
    )
    x_part = jnp.concatenate([x_part, pltpu.roll(x_part, 64, 1)], axis=0)
    place = iota((SP, LANES), 1)
    values = jnp.where(place < 64, x_part, jnp.where(place < 96, side_part, 0.0))
    basis[0] = stage[...] + diffuse * exact_dot(values, coarse_spread, 3)

    half = species // 2

    def apply_inverse(v):
        for x in range(2):
            for ct in range(2):
                part = v[0:ROWS, (2 * x + ct) * LANES : (2 * x + ct + 1) * LANES]
                even[pl.ds(2 * ct + x, ROWS, stride=4), :] = part
                odd[pl.ds(4 + 2 * ct + x, ROWS, stride=4), :] = part
        rows = 4 * species + 4
        low_half = iota((8, LANES), 0) < 4

        def product(at, vector):
            p = (wide[pl.ds(pl.multiple_of(at, 8), rows), :] * vector).reshape(
                rows // 8, 8, LANES
            )
            parts = [p[i] for i in range(rows // 8)]
            while len(parts) > 1:
                pairs = [a + c for a, c in zip(parts[0::2], parts[1::2])]
                parts = pairs + ([parts[-1]] if len(parts) % 2 else [])
            return parts[0] + pltpu.roll(parts[0], 4, 0)

        def sweep(count, start, vector, store):
            def step(m, carry):
                store(m, product(m * (8 * species) + start, vector))
                return carry

            def four(m, carry):
                for i in range(4):
                    step(4 * m + i, carry)
                return carry

            lax.fori_loop(0, count // 4, four, 0)
            for m in range(count // 4 * 4, count):
                step(m, 0)

        def store_even(m, value):
            applied[pl.ds(pl.multiple_of(m * 8, 8), 8), :] = value

        def store_odd(m, value):
            at = pl.ds(pl.multiple_of(m * 8, 8), 8)
            applied[at, :] = jnp.where(low_half, applied[at, :], value)

        sweep(half + 1, 0, even[0:rows, :], store_even)
        sweep(half, 4 * species - 4, odd[0:rows, :], store_odd)
        tail_at = pl.ds(8 * half, 8)
        applied[tail_at, :] = jnp.where(low_half, applied[tail_at, :], 0.0)
        return [
            padded(applied[pl.ds(2 * ct + x, ROWS, stride=4), :])
            for x in range(2)
            for ct in range(2)
        ]

    lane = iota((16, LANES), 1)
    wide_lane = iota((SP, LANES), 1)
    links = [neighbours[f, g] for f in range(4)]

    def rolled(x, shift):
        shift = shift % LANES
        return pltpu.roll(x, shift, 1) if shift else x

    def side_messages(flat, at):
        planes = exact_dot(flat, pick[...], 2)
        packed = []
        for f in range(4):
            total = jnp.zeros((16, LANES), F32)
            for q in range(4):
                rows = planes[16 * q : 16 * q + 16]
                total = jnp.where((lane >> 5) == q, rolled(rows, 32 * (q - f)), total)
            packed.append(total)
        for k in range(1, groups):
            peer = lax.rem(g + k, groups)
            message = jnp.zeros((16, LANES), F32)
            for f in range(4):
                message = jnp.where(links[f] == peer, packed[f], message)
            plane_send[at, k - 1] = message

    def side_ghosts(at):
        found = [jnp.zeros((16, LANES), F32)] * 4
        for k in range(1, groups):
            peer = lax.rem(g + groups - k, groups)
            message = plane_recv[at, k - 1]
            found = [
                jnp.where(links[f] == peer, message, found[f]) for f in range(4)
            ]
        rows = []
        for q in range(4):
            total = jnp.zeros((16, LANES), F32)
            for f in range(4):
                total = jnp.where((lane >> 5) == f, rolled(found[f], 32 * (f - q)), total)
            rows.append(total)
        return exact_dot(jnp.concatenate(rows, axis=0), spread[...], 2)

    def inner_sum(d):
        result = []
        zero = jnp.zeros((SP, LANES), F32)
        z = wide_lane & 15
        for x in range(2):
            plane = d[2 * x : 2 * x + 2]
            up = [rolled(p, -16) for p in plane]
            down = [rolled(p, 16) for p in plane]
            for ct in range(2):
                own = plane[ct]
                total = d[2 * (1 - x) + ct]
                total = total + jnp.where(z == 15, 0.0, rolled(own, -1))
                total = total + jnp.where(z == 0, 0.0, rolled(own, 1))
                total = total + jnp.where(wide_lane >= 112, up[1] if ct == 0 else zero, up[ct])
                total = total + jnp.where(wide_lane < 16, down[0] if ct == 1 else zero, down[ct])
                result.append(total)
        return result

    def row_of(a, c):
        p = a * c
        p = p[:, 0:128] + p[:, 128:256] + p[:, 256:384] + p[:, 384:512]
        return jnp.sum(p, axis=0, keepdims=True)

    def reduce_stage(tile, turn, stage_id):
        at = turn % 2
        first, size, peer = ((0, boxes, box_peer), (boxes - 1, groups, grp_peer))[stage_id]
        high = tile.shape[0]
        red_send[at, stage_id, 0:high] = tile
        copies = [
            remote(red_send.at[at, stage_id, 0:high], red_recv.at[at, first + k - 1, 0:high],
                   red_ssem.at[at, stage_id], red_rsem.at[at, stage_id], peer(k))
            for k in range(1, size)
        ]
        for copy in copies:
            copy.start()

        def finish():
            total = tile
            arrived = red_recv.at[at, first : first + size - 1, 0:high]
            wait_bytes(arrived, red_rsem.at[at, stage_id])
            for k in range(1, size):
                total = total + red_recv[at, first + k - 1, 0:high]
            wait_bytes(arrived, red_ssem.at[at, stage_id])
            return total

        return finish

    def reduce_rows(rows, turn):
        high = -(-len(rows) // 8) * 8
        row_id = iota((high, LANES), 0)
        tile = jnp.zeros((high, LANES), F32)
        for i, row in enumerate(rows):
            tile = jnp.where(row_id == i, row, tile)
        return reduce_stage(tile, turn, 0)

    def sums_of(tile):
        return jnp.sum(tile, axis=1, keepdims=True)

    def send_halo(v, turn):
        at = turn % 2
        d = apply_inverse(v)
        for k in range(4):
            x_send[at, k] = d[k]
        up = remote(x_send.at[at, 2:4, 0:ROWS], x_recv.at[at, 0], x_ssem.at[at, 0],
                    x_rsem.at[at, 0], (g, lax.rem(b + 1, boxes)))
        down = remote(x_send.at[at, 0:2, 0:ROWS], x_recv.at[at, 1], x_ssem.at[at, 1],
                      x_rsem.at[at, 1], (g, lax.rem(b + boxes - 1, boxes)))
        pl.when(b < boxes - 1)(up.start)
        pl.when(b > 0)(down.start)
        flat = jnp.concatenate(d, axis=1)
        side_messages(flat, at)
        plane_copies = [
            remote(plane_send.at[at, k - 1], plane_recv.at[at, k - 1], plane_ssem.at[at],
                   plane_rsem.at[at], grp_peer(k))
            for k in range(1, groups)
        ]
        for copy in plane_copies:
            copy.start()

        def finish():
            d_high, d_low = split(flat, 2)
            d_cat = jnp.concatenate([d_high, d_high, d_low, jnp.zeros_like(d_low)], axis=0)
            progress = rate[...] * dot(order_parts, d_cat)
            q_high, q_low = split(progress, 2)
            both = dot(stoich_cat[...], q_high)
            chemistry = both[0:SP] + both[SP:] + dot(stoich_cat[0:SP, :], q_low)
            inner = jnp.concatenate(inner_sum(d), axis=1)
            image = flat + diffuse * (6.0 * flat - inner) - chemistry
            pl.when(b > 0)(up.wait_recv)
            pl.when(b < boxes - 1)(down.wait_recv)
            zero = jnp.zeros((ROWS, LANES), F32)
            outer = [padded(jnp.where(b > 0, x_recv[at, 0, ct], zero)) for ct in range(2)]
            outer += [
                padded(jnp.where(b < boxes - 1, x_recv[at, 1, ct], zero)) for ct in range(2)
            ]
            wait_bytes(plane_recv.at[at], plane_rsem.at[at])
            image = image - diffuse * (jnp.concatenate(outer, axis=1) + side_ghosts(at))
            pl.when(b < boxes - 1)(up.wait_send)
            pl.when(b > 0)(down.wait_send)
            wait_bytes(plane_send.at[at], plane_ssem.at[at])
            return image

        return flat, finish

    wait_ghosts(ghost_send, ghost_ssem)

    direct[0], finish = send_halo(basis[0], 0)
    images[0] = finish()
    gram = {}
    squares = []
    lengths = []
    columns = []
    for j in range(ITERS):
        more = j + 1 < ITERS
        image = images[j]
        known = [basis[i] for i in range(j + 1)]
        rows = [row_of(known[j], known[j])] + [row_of(v, image) for v in known]
        rows += [row_of(v, known[j]) for v in known[:j]]
        if not more:
            rows.append(row_of(image, image))
        box_sums = reduce_rows(rows, j)
        if more:
            ahead, finish = send_halo(image, j + 1)
        all_sums = reduce_stage(box_sums(), j, 1)
        if more:
            ahead_image = finish()
        else:
            cell = iota((256, LANES), 0)
            slot = iota((256, LANES), 1) & 63
            to_slot = ((((cell >> 7) << 3) + ((cell & 127) >> 4)) >> 1) << 3
            to_slot = ones_where(to_slot + ((cell & 15) >> 1) == slot)
            means = []
            for i in range(ITERS):
                folded = direct[i, :, 0:256] + direct[i, :, 256:512]
                mean = exact_dot(folded, to_slot, 3) * 0.125
                means.append(jnp.where(left, mean[0:32], mean[32:64]))
        sums = sums_of(all_sums())
        sums = [sums[i : i + 1] for i in range(len(rows))]
        squares.append(sums[0])
        lengths.append(jnp.sqrt(sums[0]))
        columns.append([sums[1 + i] / (lengths[i] * lengths[j]) for i in range(j + 1)])
        for i in range(j):
            gram[i, j] = sums[j + 2 + i]
        parts = [sums[1 + i] / (squares[i] * lengths[j]) for i in range(j + 1)]
        scale = 1.0 / lengths[j]

        def corrected(field, past):
            field = field * scale
            for i in range(j + 1):
                field = field - parts[i] * past[i]
            return field

        if more:
            basis[j + 1] = corrected(image, known)
            direct[j + 1] = corrected(ahead, [direct[i] for i in range(j + 1)])
            images[j + 1] = corrected(ahead_image, [images[i] for i in range(j + 1)])

    ratios = [sums[1 + i] / squares[i] for i in range(ITERS)]
    square = sums[-1]
    for i in range(ITERS):
        square = square - ratios[i] * sums[1 + i]
    for (i, k), entry in gram.items():
        square = square + 2.0 * ratios[i] * ratios[k] * entry
    length = jnp.sqrt(jnp.maximum(square, 0.0)) / lengths[ITERS - 1]
    for j in range(ITERS):
        columns[j].append((lengths + [length])[j + 1])
    weights = least_squares(columns, lengths[0])
    scales = [weights[j] / lengths[j] for j in range(ITERS)]
    mean_send[...] = sum(scales[j] * means[j] for j in range(ITERS))
    mean_copies = [
        remote(mean_send, mean_recv.at[k - 1], mean_ssem, mean_rsem, grp_peer(k))
        for k in range(1, groups)
    ]
    for copy in mean_copies:
        copy.start()
    total = sum(scales[j] * direct[j] for j in range(ITERS))
    for x in range(2):
        for ct in range(2):
            k = 2 * x + ct
            correction_out[pl.ds(ct, species, stride=2), x, :] = total[
                0:species, k * LANES : (k + 1) * LANES
            ]
    stage[...] = jnp.zeros_like(stage)
    stage[0:species, 0:256] = coarse_raw[...]
    blocks = [stage[:, c * LANES : (c + 1) * LANES] for c in range(2)]
    wait_bytes(mean_recv, mean_rsem)
    left_half = iota((SP, LANES), 1) < 64
    for k in range(groups):
        message = mean_send[...] if k == 0 else mean_recv[k - 1]
        turned = pltpu.roll(message, 64, 1)
        message = jnp.concatenate(
            [jnp.where(left, message, turned), jnp.where(left, turned, message)], axis=0
        )
        for c in range(2):
            entry = average_list[0, lax.rem(g + groups - k, groups)] - (4 * g + 2 * c)
            blocks[c] = jnp.where(
                (left_half & (entry == 0)) | (~left_half & (entry == 1)), message, blocks[c]
            )
    for c in range(2):
        coarse_out[:, 0, c * LANES : (c + 1) * LANES] = blocks[c][0:species]
    wait_bytes(mean_recv, mean_ssem)


def hand_over(correction, updated, correction_out, updated_out, sem):
    copies = [
        pltpu.make_async_copy(correction, correction_out, sem.at[0]),
        pltpu.make_async_copy(updated, updated_out, sem.at[1]),
    ]
    for copy in copies:
        copy.start()
    for copy in copies:
        copy.wait()


def on_device(
    groups, boxes,
    source_term, diffusion, stoich, orders, rates, precond, coarse_field,
    neighbours, ghost_list, average_list,
):
    species = source_term.shape[0]
    reactions = rates.shape[0]

    def rows_of(x):
        lead = x.shape[:-3]
        x = x.reshape(lead + (2, 2, LANES))
        n = len(lead)
        x = x.transpose(tuple(range(n)) + (n + 1, n, n + 2))
        return x.reshape(-1, 2, LANES)

    hbm = pl.BlockSpec(memory_space=pl.ANY)
    smem = pl.BlockSpec(memory_space=pltpu.SMEM)
    count = 4 * species * species
    dma = pltpu.SemaphoreType.DMA
    reds = groups + boxes - 2
    correction, updated = pl.pallas_call(
        functools.partial(kernel, groups, boxes, species, reactions),
        out_shape=(
            jax.ShapeDtypeStruct((2 * species, 2, LANES), F32),
            jax.ShapeDtypeStruct((species, 1, 256), F32),
        ),
        in_specs=[smem, smem] + [hbm] * 8,
        out_specs=(pl.BlockSpec(memory_space=pltpu.VMEM),) * 2,
        scratch_shapes=[
            pltpu.VMEM((count, LANES), BF16),
            pltpu.VMEM((count + 4, LANES), F32),
            pltpu.VMEM((224, LANES), F32),
            pltpu.VMEM((232, LANES), F32),
            pltpu.VMEM((224, LANES), F32),
            pltpu.VMEM((ITERS, SP, 512), F32),
            pltpu.VMEM((ITERS, SP, 512), F32),
            pltpu.VMEM((ITERS + 1, SP, 512), F32),
            pltpu.VMEM((RP, 512), F32),
            pltpu.VMEM((SP, 512), F32),
            pltpu.VMEM((LANES, RP), F32),
            pltpu.VMEM((2 * SP, RP), BF16),
            pltpu.VMEM((512, LANES), BF16),
            pltpu.VMEM((LANES, 512), BF16),
            pltpu.VMEM((groups, 160), jnp.int32),
            pltpu.VMEM((groups, LANES), jnp.int32),
            pltpu.VMEM((4 * species, LANES), F32),
            pltpu.VMEM((1, species), F32),
            pltpu.VMEM((species, reactions), F32),
            pltpu.VMEM((species, reactions), F32),
            pltpu.VMEM((4 * reactions, LANES), F32),
            pltpu.VMEM((species, 256), F32),
            pltpu.VMEM((2, 4, SP, LANES), F32),
            pltpu.VMEM((groups - 1, 48, LANES), F32),
            pltpu.VMEM((groups - 1, 48, LANES), F32),
            pltpu.VMEM((2, groups - 1, 16, LANES), F32),
            pltpu.VMEM((2, groups - 1, 16, LANES), F32),
            pltpu.VMEM((2, 2, 2, ROWS, LANES), F32),
            pltpu.VMEM((2, 2, 16, LANES), F32),
            pltpu.VMEM((2, reds, 16, LANES), F32),
            pltpu.VMEM((32, LANES), F32),
            pltpu.VMEM((groups - 1, 32, LANES), F32),
            dma((8,)),
            dma,
            dma,
            dma((2,)),
            dma((2,)),
            dma((2, 2)),
            dma((2, 2)),
            dma((2, 2)),
            dma((2, 2)),
            dma,
            dma,
        ],
        compiler_params=pltpu.CompilerParams(
            collective_id=0, has_side_effects=True, vmem_limit_bytes=63 * 1024 * 1024
        ),
        name="gmres",
    )(
        neighbours.T,
        average_list.T,
        ghost_list,
        rows_of(source_term),
        diffusion.reshape(1, species),
        stoich,
        orders.T,
        rows_of(rates),
        coarse_field,
        rows_of(precond),
    )
    correction, updated = pl.pallas_call(
        hand_over,
        out_shape=(
            jax.ShapeDtypeStruct((2 * species, 2, LANES), F32),
            jax.ShapeDtypeStruct((species, 1, 256), F32),
        ),
        in_specs=[hbm] * 2,
        out_specs=(hbm,) * 2,
        scratch_shapes=[dma((2,))],
        compiler_params=pltpu.CompilerParams(vmem_limit_bytes=63 * 1024 * 1024),
        name="hand_over",
    )(correction, updated)
    correction = correction.reshape(species, 2, 2, LANES).transpose(0, 2, 1, 3)
    return (correction.reshape(species, 1, 2, 256), updated)


def solution(mesh):
    placed = (
        P(None, "grp", "box", None),
        P(),
        P(),
        P(),
        P(None, "grp", "box", None),
        P(None, None, "grp", "box", None),
        P(None, "grp", "box"),
        P(),
        P(None, "box", None),
        P(None, "box"),
    )
    return jax.shard_map(
        functools.partial(on_device, mesh.shape["grp"], mesh.shape["box"]),
        mesh=mesh,
        in_specs=placed,
        out_specs=(P(None, "grp", "box", None), P(None, "grp", "box")),
        check_vma=False,
    )
```

```python
import functools

import jax
import jax.numpy as jnp
from jax import lax
from jax.experimental import pallas as pl
from jax.experimental.pallas import tpu as pltpu
from jax.sharding import PartitionSpec as P

ITERS = 4
SP = 64
ROWS = 56
RP = 384
LANES = 128
MESH = pl.DeviceIdType.MESH
F32 = jnp.float32
BF16 = jnp.bfloat16


def least_squares(columns, beta):
    count = len(columns)
    target = [beta] + [jnp.zeros_like(beta)] * count
    rotations = []
    upper = []
    for j in range(count):
        entries = list(columns[j])
        for i in range(j):
            cosine_part, sine_part = rotations[i]
            first = cosine_part * entries[i] + sine_part * entries[i + 1]
            second = cosine_part * entries[i + 1] - sine_part * entries[i]
            entries[i] = first
            entries[i + 1] = second
        radius = jnp.sqrt(entries[j] * entries[j] + entries[j + 1] * entries[j + 1])
        cosine_part = entries[j] / radius
        sine_part = entries[j + 1] / radius
        rotations.append((cosine_part, sine_part))
        entries[j] = radius
        target[j + 1] = -sine_part * target[j]
        target[j] = cosine_part * target[j]
        upper.append(entries[: j + 1])
    result = [None] * count
    for j in reversed(range(count)):
        running = target[j]
        for k in range(j + 1, count):
            running = running - upper[k][j] * result[k]
        result[j] = running / upper[j][j]
    return result


def split(x, parts):
    pieces = []
    for _ in range(parts - 1):
        piece = x.astype(BF16)
        pieces.append(piece)
        x = x - piece.astype(F32)
    pieces.append(x.astype(BF16))
    return pieces


def dot(a, b):
    return jnp.dot(a, b, preferred_element_type=F32)


def exact_dot(x, ones, parts):
    rows = x.shape[0]
    product = dot(jnp.concatenate(split(x, parts), axis=0), ones)
    return sum(product[i * rows : (i + 1) * rows] for i in range(parts))


def iota(shape, dim):
    return lax.broadcasted_iota(jnp.int32, shape, dim)


def cell_of(index):
    k, l = index >> 7, index & 127
    return k >> 1, ((k & 1) << 3) + (l >> 4), l & 15


def on_face(face, t, y, z):
    return (
        ((face == 0) & (y == 0) & (z == t))
        | ((face == 1) & (y == 15) & (z == t))
        | ((face == 2) & (z == 0) & (y == t))
        | ((face == 3) & (z == 15) & (y == t))
    )


def ones_where(condition):
    return jnp.where(condition, 1.0, 0.0).astype(BF16)


def padded(x):
    return jnp.concatenate([x, jnp.zeros((SP - x.shape[0], x.shape[1]), F32)], axis=0)


def fields(x):
    return [x[:, k * LANES : (k + 1) * LANES] for k in range(4)]


def kernel(
    groups, boxes, species, reactions,
    neighbours, average_list, ghost_list, source, diffusion, stoich, orders, rates, coarse, precond,
    correction_out, coarse_out,
    raw, wide, even, odd, applied, direct, images, basis, rate, stage, tall, stoich_cat, pick, spread,
    lists, wanted_cells, source_raw, diffusion_raw, stoich_raw, orders_raw, rates_raw, coarse_raw,
    x_send, ghost_send, ghost_recv, plane_send, plane_recv, x_recv, red_send, red_recv,
    mean_send, mean_recv,
    load_sem, ghost_ssem, ghost_rsem, plane_ssem, plane_rsem, x_ssem, x_rsem,
    red_ssem, red_rsem, mean_ssem, mean_rsem,
):
    g = lax.axis_index("grp")
    b = lax.axis_index("box")
    used = -(-reactions // 16) * 16
    barrier = pltpu.get_barrier_semaphore()

    def grp_peer(k):
        return (lax.rem(g + k, groups), b)

    def box_peer(k):
        return (g, lax.rem(b + k, boxes))

    for k in range(1, groups):
        pl.semaphore_signal(barrier, inc=1, device_id=grp_peer(k), device_id_type=MESH)
    for k in range(1, boxes):
        pl.semaphore_signal(barrier, inc=1, device_id=box_peer(k), device_id_type=MESH)

    def remote(src, dst, ssem, rsem, device):
        return pltpu.make_async_remote_copy(
            src_ref=src, dst_ref=dst, send_sem=ssem, recv_sem=rsem,
            device_id=device, device_id_type=MESH,
        )

    def wait_bytes(ref, sem):
        pltpu.make_async_copy(ref, ref, sem).wait()

    loads = [
        pltpu.make_async_copy(src, dst, load_sem.at[i])
        for i, (src, dst) in enumerate((
            (ghost_list.at[:, 0, :], lists),
            (coarse.at[:, 0, :], coarse_raw),
            (precond.reshape(4 * species * species, LANES), raw),
            (rates.reshape(4 * reactions, LANES), rates_raw),
            (orders, orders_raw),
            (stoich, stoich_raw),
            (diffusion, diffusion_raw),
            (source.reshape(4 * species, LANES), source_raw),
        ))
    ]
    for load in loads:
        load.start()

    stage[...] = jnp.zeros_like(stage)
    even[...] = jnp.zeros_like(even)
    odd[...] = jnp.zeros_like(odd)
    applied[...] = jnp.zeros_like(applied)
    rate[...] = jnp.zeros_like(rate)
    x, y, z = cell_of(iota((512, LANES), 0))
    slot = iota((512, LANES), 1)
    pick[...] = ones_where(((slot >> 4 & 1) == x) & on_face(slot >> 5, slot & 15, y, z))
    x, y, z = cell_of(iota((LANES, 512), 1))
    slot = iota((LANES, 512), 0)
    spread[...] = ones_where(((slot >> 4 & 1) == x) & on_face(slot >> 5, slot & 15, y, z))
    end = jnp.where(b == 0, 0, 1)
    behind_x = (slot < 64) & (x == end) & (((y >> 1) << 3) + (z >> 1) == slot)
    past = slot - 64
    face = past >> 3
    t = jnp.where(face < 2, z, y)
    behind_side = (slot >= 64) & (slot < 96) & ((t >> 1) == (past & 7)) & on_face(face, t, y, z)
    coarse_spread = ones_where(behind_x | behind_side)
    loads[0].wait()
    loads[1].wait()
    stage[0:species, 0:256] = coarse_raw[...]
    x_slots = lists[:, 0:LANES]
    x_slots = jnp.where(b == 0, x_slots, pltpu.roll(x_slots, 64, 1))
    side_slots = jnp.concatenate(
        [
            jnp.full((groups, 64), -1, jnp.int32),
            lists[:, LANES : LANES + 32],
            jnp.full((groups, 32), -1, jnp.int32),
        ],
        axis=1,
    )
    wanted_cells[...] = jnp.where(iota((groups, LANES), 1) < 64, x_slots, side_slots)
    patch = jnp.concatenate(split(stage[:, 0:256], 3), axis=0)
    cell = iota((256, LANES), 0) + g * 256

    at_end = (b == 0) | (b == boxes - 1)
    short = iota((16, LANES), 1)
    left = iota((32, LANES), 1) < 64

    def chosen(k):
        wanted = wanted_cells[pl.ds(lax.rem(g + k, groups), 1), :]
        got = dot(patch, ones_where(cell == wanted))
        got = got[0:SP] + got[SP : 2 * SP] + got[2 * SP :]
        side_part = got[0:16]
        side_part = pltpu.roll(side_part, 64, 1)
        for q in range(1, 4):
            rows = got[16 * q : 16 * q + 16]
            rows = rows if q == 2 else pltpu.roll(rows, (32 * q - 64) % LANES, 1)
            side_part = jnp.where((short >> 5) == q, rows, side_part)
        x_part = jnp.where(left, got[0:32], pltpu.roll(got[32:64], 64, 1))
        return jnp.concatenate([side_part, x_part], axis=0)

    for k in range(1, groups):
        ghost_send[k - 1] = chosen(k)
    pl.semaphore_wait(barrier, groups + boxes - 2)

    def ghost_copies(rows):
        return [
            remote(ghost_send.at[k - 1, 0:rows], ghost_recv.at[k - 1, 0:rows],
                   ghost_ssem, ghost_rsem, grp_peer(k))
            for k in range(1, groups)
        ]

    def start_ghosts(rows):
        for copy in ghost_copies(rows):
            copy.start()

    def wait_ghosts(ref, sem):
        pl.when(at_end)(lambda: wait_bytes(ref.at[:, 0:48], sem))
        pl.when(jnp.logical_not(at_end))(lambda: wait_bytes(ref.at[:, 0:16], sem))

    pl.when(at_end)(lambda: start_ghosts(48))
    pl.when(jnp.logical_not(at_end))(lambda: start_ghosts(16))
    own_ghosts = chosen(0)

    for load in loads[3:]:
        load.wait()
    for x in range(2):
        for ct in range(2):
            k = 2 * x + ct
            rate[0:reactions, k * LANES : (k + 1) * LANES] = rates_raw[
                pl.ds(2 * ct + x, reactions, stride=4), :
            ]
    tall[...] = jnp.zeros_like(tall)
    tall[0:species, 0:reactions] = orders_raw[...]
    whole = tall[...].T
    high = whole.astype(BF16).astype(F32)
    low = whole - high
    order_parts = jnp.concatenate([high + pltpu.roll(low, 64, 1), high], axis=1)[0:used].astype(BF16)
    stage[...] = jnp.zeros_like(stage)
    stage[0:species, 0:reactions] = stoich_raw[...]
    whole = stage[:, 0:RP]
    stoich_high, stoich_low = split(whole, 2)
    stoich_cat[0:SP, :] = stoich_high
    stoich_cat[SP : 2 * SP, :] = stoich_low
    loads[2].wait()
    count = species * species * 4
    chunk = 432
    steps = count // chunk

    def widen(i, carry):
        at = pl.multiple_of(i * chunk, 16)
        wide[pl.ds(at, chunk), :] = raw[pl.ds(at, chunk), :].astype(F32)
        return carry

    lax.fori_loop(0, steps, widen, 0)
    tail = steps * chunk
    wide[tail:, :] = jnp.zeros((wide.shape[0] - tail, LANES), F32)
    wide[tail:count, :] = raw[tail:count, :].astype(F32)

    tall[0:8, 0:LANES] = jnp.zeros((8, LANES), F32)
    tall[0:1, 0:species] = diffusion_raw[...]
    same = iota((SP, LANES), 0) == iota((SP, LANES), 1)
    diffuse = jnp.sum(jnp.where(same, tall[0:1, 0:LANES], 0.0), axis=1, keepdims=True)
    diffuse = jnp.broadcast_to(diffuse, (SP, 512))
    stage[...] = jnp.zeros_like(stage)
    for x in range(2):
        for ct in range(2):
            k = 2 * x + ct
            stage[0:species, k * LANES : (k + 1) * LANES] = source_raw[
                pl.ds(2 * ct + x, species, stride=4), :
            ]
    wait_ghosts(ghost_recv, ghost_rsem)
    side_part = own_ghosts[0:16]
    x_part = jnp.where(at_end, own_ghosts[16:48], 0.0)
    for k in range(1, groups):
        side_part = side_part + ghost_recv[k - 1, 0:16]
        x_part = x_part + jnp.where(at_end, ghost_recv[k - 1, 16:48], 0.0)
    side_part = jnp.concatenate(
        [
            pltpu.roll(side_part, 64, 1),
            pltpu.roll(side_part, 32, 1),
            side_part,
            pltpu.roll(side_part, 96, 1),
        ],
        axis=0,
    )
    x_part = jnp.concatenate([x_part, pltpu.roll(x_part, 64, 1)], axis=0)
    place = iota((SP, LANES), 1)
    values = jnp.where(place < 64, x_part, jnp.where(place < 96, side_part, 0.0))
    basis[0] = stage[...] + diffuse * exact_dot(values, coarse_spread, 3)

    half = species // 2

    def apply_inverse(v):
        for x in range(2):
            for ct in range(2):
                part = v[0:ROWS, (2 * x + ct) * LANES : (2 * x + ct + 1) * LANES]
                even[pl.ds(2 * ct + x, ROWS, stride=4), :] = part
                odd[pl.ds(4 + 2 * ct + x, ROWS, stride=4), :] = part
        rows = 4 * species + 4
        low_half = iota((8, LANES), 0) < 4

        def product(at, vector):
            p = (wide[pl.ds(pl.multiple_of(at, 8), rows), :] * vector).reshape(
                rows // 8, 8, LANES
            )
            parts = [p[i] for i in range(rows // 8)]
            while len(parts) > 1:
                pairs = [a + c for a, c in zip(parts[0::2], parts[1::2])]
                parts = pairs + ([parts[-1]] if len(parts) % 2 else [])
            return parts[0] + pltpu.roll(parts[0], 4, 0)

        def sweep(count, start, vector, store):
            def step(m, carry):
                store(m, product(m * (8 * species) + start, vector))
                return carry

            def four(m, carry):
                for i in range(4):
                    step(4 * m + i, carry)
                return carry

            lax.fori_loop(0, count // 4, four, 0)
            for m in range(count // 4 * 4, count):
                step(m, 0)

        def store_even(m, value):
            applied[pl.ds(pl.multiple_of(m * 8, 8), 8), :] = value

        def store_odd(m, value):
            at = pl.ds(pl.multiple_of(m * 8, 8), 8)
            applied[at, :] = jnp.where(low_half, applied[at, :], value)

        sweep(half + 1, 0, even[0:rows, :], store_even)
        sweep(half, 4 * species - 4, odd[0:rows, :], store_odd)
        tail_at = pl.ds(8 * half, 8)
        applied[tail_at, :] = jnp.where(low_half, applied[tail_at, :], 0.0)
        return [
            padded(applied[pl.ds(2 * ct + x, ROWS, stride=4), :])
            for x in range(2)
            for ct in range(2)
        ]

    lane = iota((16, LANES), 1)
    wide_lane = iota((SP, LANES), 1)
    links = [neighbours[f, g] for f in range(4)]

    def rolled(x, shift):
        shift = shift % LANES
        return pltpu.roll(x, shift, 1) if shift else x

    def side_messages(flat, at):
        planes = exact_dot(flat, pick[...], 2)
        packed = []
        for f in range(4):
            total = jnp.zeros((16, LANES), F32)
            for q in range(4):
                rows = planes[16 * q : 16 * q + 16]
                total = jnp.where((lane >> 5) == q, rolled(rows, 32 * (q - f)), total)
            packed.append(total)
        for k in range(1, groups):
            peer = lax.rem(g + k, groups)
            message = jnp.zeros((16, LANES), F32)
            for f in range(4):
                message = jnp.where(links[f] == peer, packed[f], message)
            plane_send[at, k - 1] = message

    def side_ghosts(at):
        found = [jnp.zeros((16, LANES), F32)] * 4
        for k in range(1, groups):
            peer = lax.rem(g + groups - k, groups)
            message = plane_recv[at, k - 1]
            found = [
                jnp.where(links[f] == peer, message, found[f]) for f in range(4)
            ]
        rows = []
        for q in range(4):
            total = jnp.zeros((16, LANES), F32)
            for f in range(4):
                total = jnp.where((lane >> 5) == f, rolled(found[f], 32 * (f - q)), total)
            rows.append(total)
        return exact_dot(jnp.concatenate(rows, axis=0), spread[...], 2)

    def inner_sum(d):
        result = []
        zero = jnp.zeros((SP, LANES), F32)
        z = wide_lane & 15
        for x in range(2):
            plane = d[2 * x : 2 * x + 2]
            up = [rolled(p, -16) for p in plane]
            down = [rolled(p, 16) for p in plane]
            for ct in range(2):
                own = plane[ct]
                total = d[2 * (1 - x) + ct]
                total = total + jnp.where(z == 15, 0.0, rolled(own, -1))
                total = total + jnp.where(z == 0, 0.0, rolled(own, 1))
                total = total + jnp.where(wide_lane >= 112, up[1] if ct == 0 else zero, up[ct])
                total = total + jnp.where(wide_lane < 16, down[0] if ct == 1 else zero, down[ct])
                result.append(total)
        return result

    def row_of(a, c):
        p = a * c
        p = p[:, 0:128] + p[:, 128:256] + p[:, 256:384] + p[:, 384:512]
        return jnp.sum(p, axis=0, keepdims=True)

    def reduce_stage(tile, turn, stage_id):
        at = turn % 2
        first, size, peer = ((0, boxes, box_peer), (boxes - 1, groups, grp_peer))[stage_id]
        high = tile.shape[0]
        red_send[at, stage_id, 0:high] = tile
        copies = [
            remote(red_send.at[at, stage_id, 0:high], red_recv.at[at, first + k - 1, 0:high],
                   red_ssem.at[at, stage_id], red_rsem.at[at, stage_id], peer(k))
            for k in range(1, size)
        ]
        for copy in copies:
            copy.start()

        def finish():
            total = tile
            arrived = red_recv.at[at, first : first + size - 1, 0:high]
            wait_bytes(arrived, red_rsem.at[at, stage_id])
            for k in range(1, size):
                total = total + red_recv[at, first + k - 1, 0:high]
            wait_bytes(arrived, red_ssem.at[at, stage_id])
            return total

        return finish

    def reduce_rows(rows, turn):
        high = -(-len(rows) // 8) * 8
        row_id = iota((high, LANES), 0)
        tile = jnp.zeros((high, LANES), F32)
        for i, row in enumerate(rows):
            tile = jnp.where(row_id == i, row, tile)
        return reduce_stage(tile, turn, 0)

    def sums_of(tile):
        return jnp.sum(tile, axis=1, keepdims=True)

    def send_halo(v, turn):
        at = turn % 2
        d = apply_inverse(v)
        for k in range(4):
            x_send[at, k] = d[k]
        up = remote(x_send.at[at, 2:4, 0:ROWS], x_recv.at[at, 0], x_ssem.at[at, 0],
                    x_rsem.at[at, 0], (g, lax.rem(b + 1, boxes)))
        down = remote(x_send.at[at, 0:2, 0:ROWS], x_recv.at[at, 1], x_ssem.at[at, 1],
                      x_rsem.at[at, 1], (g, lax.rem(b + boxes - 1, boxes)))
        pl.when(b < boxes - 1)(up.start)
        pl.when(b > 0)(down.start)
        flat = jnp.concatenate(d, axis=1)
        side_messages(flat, at)
        plane_copies = [
            remote(plane_send.at[at, k - 1], plane_recv.at[at, k - 1], plane_ssem.at[at],
                   plane_rsem.at[at], grp_peer(k))
            for k in range(1, groups)
        ]
        for copy in plane_copies:
            copy.start()

        def finish():
            d_high, d_low = split(flat, 2)
            d_cat = jnp.concatenate([d_high, d_high, d_low, jnp.zeros_like(d_low)], axis=0)
            progress = rate[0:used, :] * dot(order_parts, d_cat)
            q_high, q_low = split(progress, 2)
            both = dot(stoich_cat[:, 0:used], q_high)
            chemistry = both[0:SP] + both[SP:] + dot(stoich_cat[0:SP, 0:used], q_low)
            inner = jnp.concatenate(inner_sum(d), axis=1)
            image = flat + diffuse * (6.0 * flat - inner) - chemistry
            pl.when(b > 0)(up.wait_recv)
            pl.when(b < boxes - 1)(down.wait_recv)
            zero = jnp.zeros((ROWS, LANES), F32)
            outer = [padded(jnp.where(b > 0, x_recv[at, 0, ct], zero)) for ct in range(2)]
            outer += [
                padded(jnp.where(b < boxes - 1, x_recv[at, 1, ct], zero)) for ct in range(2)
            ]
            wait_bytes(plane_recv.at[at], plane_rsem.at[at])
            image = image - diffuse * (jnp.concatenate(outer, axis=1) + side_ghosts(at))
            pl.when(b < boxes - 1)(up.wait_send)
            pl.when(b > 0)(down.wait_send)
            wait_bytes(plane_send.at[at], plane_ssem.at[at])
            return image

        return flat, finish

    wait_ghosts(ghost_send, ghost_ssem)

    direct[0], finish = send_halo(basis[0], 0)
    images[0] = finish()
    gram = {}
    squares = []
    lengths = []
    columns = []
    for j in range(ITERS):
        more = j + 1 < ITERS
        image = images[j]
        known = [basis[i] for i in range(j + 1)]
        rows = [row_of(known[j], known[j])] + [row_of(v, image) for v in known]
        rows += [row_of(v, known[j]) for v in known[:j]]
        if not more:
            rows.append(row_of(image, image))
        box_sums = reduce_rows(rows, j)
        if more:
            ahead, finish = send_halo(image, j + 1)
        all_sums = reduce_stage(box_sums(), j, 1)
        if more:
            ahead_image = finish()
        else:
            cell = iota((256, LANES), 0)
            slot = iota((256, LANES), 1) & 63
            to_slot = ((((cell >> 7) << 3) + ((cell & 127) >> 4)) >> 1) << 3
            to_slot = ones_where(to_slot + ((cell & 15) >> 1) == slot)
            means = []
            for i in range(ITERS):
                folded = direct[i, :, 0:256] + direct[i, :, 256:512]
                mean = exact_dot(folded, to_slot, 3) * 0.125
                means.append(jnp.where(left, mean[0:32], mean[32:64]))
        sums = sums_of(all_sums())
        sums = [sums[i : i + 1] for i in range(len(rows))]
        squares.append(sums[0])
        lengths.append(jnp.sqrt(sums[0]))
        columns.append([sums[1 + i] / (lengths[i] * lengths[j]) for i in range(j + 1)])
        for i in range(j):
            gram[i, j] = sums[j + 2 + i]
        parts = [sums[1 + i] / (squares[i] * lengths[j]) for i in range(j + 1)]
        scale = 1.0 / lengths[j]

        def corrected(field, past):
            field = field * scale
            for i in range(j + 1):
                field = field - parts[i] * past[i]
            return field

        if more:
            basis[j + 1] = corrected(image, known)
            direct[j + 1] = corrected(ahead, [direct[i] for i in range(j + 1)])
            images[j + 1] = corrected(ahead_image, [images[i] for i in range(j + 1)])

    ratios = [sums[1 + i] / squares[i] for i in range(ITERS)]
    square = sums[-1]
    for i in range(ITERS):
        square = square - ratios[i] * sums[1 + i]
    for (i, k), entry in gram.items():
        square = square + 2.0 * ratios[i] * ratios[k] * entry
    length = jnp.sqrt(jnp.maximum(square, 0.0)) / lengths[ITERS - 1]
    for j in range(ITERS):
        columns[j].append((lengths + [length])[j + 1])
    weights = least_squares(columns, lengths[0])
    scales = [weights[j] / lengths[j] for j in range(ITERS)]
    mean_send[...] = sum(scales[j] * means[j] for j in range(ITERS))
    mean_copies = [
        remote(mean_send, mean_recv.at[k - 1], mean_ssem, mean_rsem, grp_peer(k))
        for k in range(1, groups)
    ]
    for copy in mean_copies:
        copy.start()
    total = sum(scales[j] * direct[j] for j in range(ITERS))
    for x in range(2):
        for ct in range(2):
            k = 2 * x + ct
            correction_out[pl.ds(ct, species, stride=2), x, :] = total[
                0:species, k * LANES : (k + 1) * LANES
            ]
    stage[...] = jnp.zeros_like(stage)
    stage[0:species, 0:256] = coarse_raw[...]
    blocks = [stage[:, c * LANES : (c + 1) * LANES] for c in range(2)]
    wait_bytes(mean_recv, mean_rsem)
    left_half = iota((SP, LANES), 1) < 64
    for k in range(groups):
        message = mean_send[...] if k == 0 else mean_recv[k - 1]
        turned = pltpu.roll(message, 64, 1)
        message = jnp.concatenate(
            [jnp.where(left, message, turned), jnp.where(left, turned, message)], axis=0
        )
        for c in range(2):
            entry = average_list[0, lax.rem(g + groups - k, groups)] - (4 * g + 2 * c)
            blocks[c] = jnp.where(
                (left_half & (entry == 0)) | (~left_half & (entry == 1)), message, blocks[c]
            )
    for c in range(2):
        coarse_out[:, 0, c * LANES : (c + 1) * LANES] = blocks[c][0:species]
    wait_bytes(mean_recv, mean_ssem)


def hand_over(correction, updated, correction_out, updated_out, held, held_patch, sem):
    inward = [
        pltpu.make_async_copy(correction, held, sem.at[0]),
        pltpu.make_async_copy(updated, held_patch, sem.at[1]),
    ]
    outward = [
        pltpu.make_async_copy(held, correction_out, sem.at[2]),
        pltpu.make_async_copy(held_patch, updated_out, sem.at[3]),
    ]
    for copy in inward:
        copy.start()
    for copy, following in zip(inward, outward):
        copy.wait()
        following.start()
    for copy in outward:
        copy.wait()


def on_device(
    groups, boxes,
    source_term, diffusion, stoich, orders, rates, precond, coarse_field,
    neighbours, ghost_list, average_list,
):
    species = source_term.shape[0]
    reactions = rates.shape[0]

    def rows_of(x):
        lead = x.shape[:-3]
        x = x.reshape(lead + (2, 2, LANES))
        n = len(lead)
        x = x.transpose(tuple(range(n)) + (n + 1, n, n + 2))
        return x.reshape(-1, 2, LANES)

    hbm = pl.BlockSpec(memory_space=pl.ANY)
    smem = pl.BlockSpec(memory_space=pltpu.SMEM)
    count = 4 * species * species
    dma = pltpu.SemaphoreType.DMA
    reds = groups + boxes - 2
    correction, updated = pl.pallas_call(
        functools.partial(kernel, groups, boxes, species, reactions),
        out_shape=(
            jax.ShapeDtypeStruct((2 * species, 2, LANES), F32),
            jax.ShapeDtypeStruct((species, 1, 256), F32),
        ),
        in_specs=[smem, smem] + [hbm] * 8,
        out_specs=(pl.BlockSpec(memory_space=pltpu.VMEM),) * 2,
        scratch_shapes=[
            pltpu.VMEM((count, LANES), BF16),
            pltpu.VMEM((count + 4, LANES), F32),
            pltpu.VMEM((224, LANES), F32),
            pltpu.VMEM((232, LANES), F32),
            pltpu.VMEM((224, LANES), F32),
            pltpu.VMEM((ITERS, SP, 512), F32),
            pltpu.VMEM((ITERS, SP, 512), F32),
            pltpu.VMEM((ITERS + 1, SP, 512), F32),
            pltpu.VMEM((RP, 512), F32),
            pltpu.VMEM((SP, 512), F32),
            pltpu.VMEM((LANES, RP), F32),
            pltpu.VMEM((2 * SP, RP), BF16),
            pltpu.VMEM((512, LANES), BF16),
            pltpu.VMEM((LANES, 512), BF16),
            pltpu.VMEM((groups, 160), jnp.int32),
            pltpu.VMEM((groups, LANES), jnp.int32),
            pltpu.VMEM((4 * species, LANES), F32),
            pltpu.VMEM((1, species), F32),
            pltpu.VMEM((species, reactions), F32),
            pltpu.VMEM((species, reactions), F32),
            pltpu.VMEM((4 * reactions, LANES), F32),
            pltpu.VMEM((species, 256), F32),
            pltpu.VMEM((2, 4, SP, LANES), F32),
            pltpu.VMEM((groups - 1, 48, LANES), F32),
            pltpu.VMEM((groups - 1, 48, LANES), F32),
            pltpu.VMEM((2, groups - 1, 16, LANES), F32),
            pltpu.VMEM((2, groups - 1, 16, LANES), F32),
            pltpu.VMEM((2, 2, 2, ROWS, LANES), F32),
            pltpu.VMEM((2, 2, 16, LANES), F32),
            pltpu.VMEM((2, reds, 16, LANES), F32),
            pltpu.VMEM((32, LANES), F32),
            pltpu.VMEM((groups - 1, 32, LANES), F32),
            dma((8,)),
            dma,
            dma,
            dma((2,)),
            dma((2,)),
            dma((2, 2)),
            dma((2, 2)),
            dma((2, 2)),
            dma((2, 2)),
            dma,
            dma,
        ],
        compiler_params=pltpu.CompilerParams(
            collective_id=0, has_side_effects=True, vmem_limit_bytes=63 * 1024 * 1024
        ),
        name="gmres",
    )(
        neighbours.T,
        average_list.T,
        ghost_list,
        rows_of(source_term),
        diffusion.reshape(1, species),
        stoich,
        orders.T,
        rows_of(rates),
        coarse_field,
        rows_of(precond),
    )
    correction, updated = pl.pallas_call(
        hand_over,
        out_shape=(
            jax.ShapeDtypeStruct((2 * species, 2, LANES), F32),
            jax.ShapeDtypeStruct((species, 1, 256), F32),
        ),
        in_specs=[hbm] * 2,
        out_specs=(hbm,) * 2,
        scratch_shapes=[
            pltpu.VMEM((2 * species, 2, LANES), F32),
            pltpu.VMEM((species, 1, 256), F32),
            dma((4,)),
        ],
        compiler_params=pltpu.CompilerParams(vmem_limit_bytes=63 * 1024 * 1024),
        name="hand_over",
    )(correction, updated)
    correction = correction.reshape(species, 2, 2, LANES).transpose(0, 2, 1, 3)
    return (correction.reshape(species, 1, 2, 256), updated)


def solution(mesh):
    placed = (
        P(None, "grp", "box", None),
        P(),
        P(),
        P(),
        P(None, "grp", "box", None),
        P(None, None, "grp", "box", None),
        P(None, "grp", "box"),
        P(),
        P(None, "box", None),
        P(None, "box"),
    )
    return jax.shard_map(
        functools.partial(on_device, mesh.shape["grp"], mesh.shape["box"]),
        mesh=mesh,
        in_specs=placed,
        out_specs=(P(None, "grp", "box", None), P(None, "grp", "box")),
        check_vma=False,
    )
```
